256 devices in a mesh: dp: 16 (over z_lo, y, core), tensor: 16 (over x, z_hi).
Axes of the slice: x: 4, y: 4, z: 8 (z_hi: 4, z_lo: 2; z = z_hi * 2 + z_lo), core: 2. Of those that a mesh axis runs over, the one named last changes fastest.
Arguments:
- tokens: bfloat16 [4096, 6144], P(('dp', 'tensor')), parts along dimension 0, may hold values from -6 to 6
- norm_gain: float32 [6144], replicated, may hold values from 0.1 to 1.9
- gate_weight: bfloat16 [6144, 14336], P(None, 'tensor'), may hold values from -0.078125 to 0.078125
- up_weight: bfloat16 [6144, 14336], P(None, 'tensor'), may hold values from -0.078125 to 0.078125
- down_weight: bfloat16 [14336, 6144], P('tensor'), may hold values from -0.046875 to 0.046875
Outputs:
- block_out: bfloat16 [4096, 6144], P(('dp', 'tensor')), parts along dimension 0
The draws below stay inside these ranges and needn't reach their ends.
There are 16 independent parts, one for each index of `dp`. The reference program is written for one: setup_inputs(seed, part) draws one part's arguments, and reference() takes and returns one part's arrays. A program takes and returns all parts, laid end to end along the dimension named above; an argument that names none is the same for every part. Nothing has to cross between parts.
All inputs are finite; a program needn't handle non-finite values.
Results may differ from the reference program's by a relative error of at most 0.0051.
Values may be sent and summed in bfloat16 or wider, within the bound.
No kernel may reach another device: no remote copies, remote signals or barrier semaphores. Data moves between devices by JAX's collectives and lax.ppermute only.
A program may use at most 128 MiB of HBM per device.

```python
import jax
import jax.numpy as jnp
from jax import lax

D = 6144
FF = 14336
ROWS = 256


def block_levels(rng, shape, shards, smallest, largest):
    def one(position, shards_of):
        heights = jax.random.uniform(jax.random.fold_in(jax.random.fold_in(rng, 6), position), (shards_of,), jnp.float32, smallest / len(shards), largest / len(shards))
        return jnp.repeat(jnp.exp(heights), shape[position] // shards_of).reshape((-1,) + (1,) * (len(shape) - position - 1))

    gain = one(*shards[0])
    for cut in shards[1:]:
        gain = gain * one(*cut)
    return gain


def gaussian(key, extent, deviation, most, pieces=(), held_as=jnp.bfloat16):
    entries = jax.random.normal(key, extent, jnp.float32) * deviation
    if len(pieces) > 0:
        entries = block_levels(key, extent, pieces, -0.22, 0.18) * entries
    return jnp.clip(entries, min=-most, max=most).astype(held_as)


def setup_inputs(seed: int = 0, part: int = 0) -> dict:
    key_of = jax.random.split(jax.random.key(seed), 6)
    own_keys = jax.random.split(jax.random.fold_in(key_of[5], part), 6)
    return {
        "tokens": gaussian(own_keys[0], (ROWS, D), 1.0, 6.0, ((0, 16),)),
        "norm_gain": jnp.clip(1.0 + 0.18 * jax.random.normal(key_of[1], (D,), jnp.float32), 0.1, 1.9),
        "gate_weight": gaussian(key_of[2], (D, FF), D ** -0.5, 0.078125, ((1, 16),)),
        "up_weight": gaussian(key_of[3], (D, FF), D ** -0.5, 0.078125, ((1, 16),)),
        "down_weight": gaussian(key_of[4], (FF, D), FF ** -0.5, 0.046875, ((0, 16),)),
    }


def reference(tokens, norm_gain, gate_weight, up_weight, down_weight):
    rows = tokens.astype(jnp.float32)
    scale = jax.lax.rsqrt(lax.optimization_barrier(jnp.mean(rows * rows, axis=1, keepdims=True)) + 1e-05)
    normed = (rows * scale * norm_gain).astype(jnp.bfloat16)
    gate = jnp.dot(normed, gate_weight, preferred_element_type=jnp.float32)
    up = jnp.dot(normed, up_weight, preferred_element_type=jnp.float32)
    hidden = (jax.nn.silu(gate) * up).astype(jnp.bfloat16)
    branch = jnp.dot(hidden, down_weight, preferred_element_type=jnp.float32)
    return (rows + branch).astype(jnp.bfloat16)
```

```python
import jax
import jax.numpy as jnp
from jax import lax
from jax.sharding import PartitionSpec as P

SIDE = 4


def shift(block, dx, dz):
    pairs = [
        (x * SIDE + z, (x + dx) % SIDE * SIDE + (z + dz) % SIDE)
        for x in range(SIDE)
        for z in range(SIDE)
    ]
    return lax.ppermute(block, "tensor", pairs)


def rms_normed(rows_in, norm_gain):
    rows = rows_in.astype(jnp.float32)
    scale = lax.rsqrt(jnp.mean(rows * rows, axis=1, keepdims=True) + 1e-05)
    return (rows * scale * norm_gain).astype(jnp.bfloat16)


def block_terms(normed, gate_weight, up_weight, down_weight):
    gate = jnp.dot(normed, gate_weight, preferred_element_type=jnp.float32)
    up = jnp.dot(normed, up_weight, preferred_element_type=jnp.float32)
    hidden = (jax.nn.silu(gate) * up).astype(jnp.bfloat16)
    return jnp.dot(hidden, down_weight, preferred_element_type=jnp.float32)


HOPS = (1, -1, 2)


def on_device(tokens, norm_gain, gate_weight, up_weight, down_weight):
    n = tokens.shape[0]
    own = rms_normed(tokens, norm_gain)
    z_near = jnp.concatenate([shift(own, 0, 1), shift(own, 0, -1)], 0)
    z_far = shift(own, 0, 2)
    sets = []
    for held in (own, z_near, z_far):
        sets.append([held] + [shift(held, d, 0) for d in HOPS])
    rows = [jnp.concatenate(s, 0) for s in sets]
    terms = block_terms(jnp.concatenate(rows, 0), gate_weight, up_weight, down_weight)
    t_own, t_near, t_far = terms[: 4 * n], terms[4 * n : 12 * n], terms[12 * n :]

    def back(t, k):
        total = t[:k]
        for i, d in enumerate(HOPS):
            total = total + shift(t[(i + 1) * k : (i + 2) * k].astype(jnp.bfloat16), -d, 0).astype(jnp.float32)
        return total

    near = back(t_near, 2 * n).astype(jnp.bfloat16)
    far = back(t_far, n).astype(jnp.bfloat16)
    mine = back(t_own, n)
    for part in (shift(near[:n], 0, -1), shift(near[n:], 0, 1), shift(far, 0, -2)):
        mine = mine + part.astype(jnp.float32)
    return (tokens.astype(jnp.float32) + mine).astype(jnp.bfloat16)


def solution(mesh):
    return jax.shard_map(
        on_device,
        mesh=mesh,
        in_specs=(
            P(("dp", "tensor"), None),
            P(),
            P(None, "tensor"),
            P(None, "tensor"),
            P("tensor", None),
        ),
        out_specs=P(("dp", "tensor"), None),
        check_vma=False,
    )
```

```python
import jax
import jax.numpy as jnp
from jax import lax
from jax.experimental import pallas as pl
from jax.experimental.pallas import tpu as pltpu
from jax.sharding import PartitionSpec as P

SIDE = 4


def shift(block, dx, dz):
    pairs = [
        (x * SIDE + z, (x + dx) % SIDE * SIDE + (z + dz) % SIDE)
        for x in range(SIDE)
        for z in range(SIDE)
    ]
    return lax.ppermute(block, "tensor", pairs)


def b16(v):
    return v.astype(jnp.bfloat16)


def f32(v):
    return v.astype(jnp.float32)


def rms_normed(rows_in, norm_gain):
    rows = f32(rows_in)
    scale = lax.rsqrt(jnp.mean(rows * rows, axis=1, keepdims=True) + 1e-05)
    return b16(rows * scale * norm_gain)


def swiglu(n, *refs):
    ins, (gate_w, up_w, down_w), outs, (rows, hidden) = refs[:15], refs[15:18], refs[18:-2], refs[-2:]
    plain, (two_up, two_down, below_2, above_2, far_2up, far_2down) = ins[:9], ins[9:]
    own_here, own_left, own_right, near_here, near_left, near_right, far_here, far_left, far_right = outs[:9]
    out_up, out_down = outs[9:]
    d = rows.shape[1]
    half = d // 2
    for ref, at in zip(plain, (0, 1, 2, 4, 5, 6, 8, 13, 14), strict=True):
        rows[at * n : at * n + ref.shape[0], :] = ref[...]
    rows[3 * n : 4 * n, :half] = two_up[:, d:]
    rows[3 * n : 4 * n, half:] = two_down[:, d:]
    rows[10 * n : 11 * n, :] = two_up[:, :d]
    rows[11 * n : 12 * n, :] = two_down[:, :d]
    rows[12 * n : 13 * n, :half] = below_2[...]
    rows[12 * n : 13 * n, half:] = above_2[...]
    rows[15 * n :, :half] = far_2up[...]
    rows[15 * n :, half:] = far_2down[...]

    def units(start, size):
        cut = pl.ds(start, size)
        gate = jnp.dot(rows[...], gate_w[:, cut], preferred_element_type=jnp.float32)
        up = jnp.dot(rows[...], up_w[:, cut], preferred_element_type=jnp.float32)
        hidden[:, cut] = b16(gate / (1.0 + jnp.exp(-gate)) * up)

    step = 1024
    units(0, gate_w.shape[1])

    def columns(start, second):
        cut = pl.ds(start, step)
        terms = jnp.dot(hidden[...], down_w[:, cut], preferred_element_type=jnp.float32)

        def part(i, k=1):
            return terms[i * n : (i + k) * n]

        own_here[:, cut] = part(0)
        near_here[:, cut] = part(4, 2)
        far_here[:, cut] = part(12)
        near_left[:, cut] = part(6, 2)
        near_right[:, cut] = part(8, 2)
        own_left[:, cut] = part(1)
        own_right[:, cut] = part(2)
        far_left[:, cut] = part(13)
        far_right[:, cut] = part(14)
        out_up[:, cut] = b16(part(10))
        out_down[:, cut] = b16(part(11))
        if second:
            out_down[:, pl.ds(start + half, step)] = b16(part(3))
            out_down[:, pl.ds(start + d, step)] = b16(part(15))
        else:
            out_up[:, pl.ds(start + d, step)] = b16(part(3))
            out_up[:, pl.ds(start + d + half, step)] = b16(part(15))

    for second in (False, True):

        @pl.loop(0, half // step)
        def _(i):
            columns(pl.multiple_of(i * step, step) + second * half, second)


def block_terms(blocks):
    n, d = blocks[0].shape
    ff = blocks[-1].shape[0]
    b, f, h = jnp.bfloat16, jnp.float32, d // 2
    shapes = [
        (n, d, f), (n, d, f), (n, d, f), (2 * n, d, f), (2 * n, d, f), (2 * n, d, f),
        (n, d, f), (n, d, f), (n, d, f), (n, 2 * d, b), (n, 2 * d, b),
    ]
    vmem = pl.BlockSpec(memory_space=pltpu.VMEM)
    return pl.pallas_call(
        lambda *refs: swiglu(n, *refs),
        out_shape=[jax.ShapeDtypeStruct(s[:2], s[2]) for s in shapes],
        in_specs=[vmem] * len(blocks),
        out_specs=[vmem] * len(shapes),
        scratch_shapes=[pltpu.VMEM((16 * n, d), b), pltpu.VMEM((16 * n, ff), b)],
        compiler_params=pltpu.CompilerParams(vmem_limit_bytes=14 * 1024 * 1024),
        cost_estimate=pl.CostEstimate(flops=6 * 16 * n * d * ff, bytes_accessed=6 * d * ff, transcendentals=16 * n * ff),
    )(*[pltpu.with_memory_space_constraint(b, pltpu.VMEM) for b in blocks])


def fetched(weight):
    def kernel(source, target, done):
        copy = pltpu.make_async_copy(source, target, done)
        copy.start()
        copy.wait()

    return pl.pallas_call(
        kernel,
        out_shape=pltpu.VMEM(weight.shape, weight.dtype),
        in_specs=[pl.BlockSpec(memory_space=pltpu.HBM)],
        out_specs=pl.BlockSpec(memory_space=pltpu.VMEM),
        scratch_shapes=[pltpu.SemaphoreType.DMA],
        compiler_params=pltpu.CompilerParams(vmem_limit_bytes=1024 * 1024),
        cost_estimate=pl.CostEstimate(flops=0, bytes_accessed=2 * weight.size, transcendentals=0),
    )(pltpu.with_memory_space_constraint(weight, pltpu.HBM))


def gathered(own, gate_weight, up_weight, down_weight):
    n, d = own.shape
    h = d // 2
    below, above = shift(own, 0, 1), shift(own, 0, -1)
    own_l, own_r = shift(own, 1, 0), shift(own, -1, 0)
    gate_weight = fetched(gate_weight)
    near, own_l, own_r, gate_weight = lax.optimization_barrier((jnp.concatenate([below, above], 0), own_l, own_r, gate_weight))
    below_2, above_2 = shift(below[:, :h], 0, 1), shift(above[:, h:], 0, -1)
    near_l, near_r = shift(near, 1, 0), shift(near, -1, 0)
    up_weight = fetched(up_weight)
    far, up_weight = lax.optimization_barrier((jnp.concatenate([below_2, above_2], 1), up_weight))
    far_l, far_r = shift(far, 1, 0), shift(far, -1, 0)
    two_up = shift(jnp.concatenate([near_l[:n], own_l[:, :h]], 1), 1, 0)
    two_down = shift(jnp.concatenate([near_r[n:], own_r[:, h:]], 1), -1, 0)
    far_2up, far_2down = shift(far_l[:, :h], 1, 0), shift(far_r[:, h:], -1, 0)
    return [
        own, own_l, own_r, below, above, near_l, near_r, far_l, far_r,
        two_up, two_down, below_2, above_2, far_2up, far_2down, gate_weight, up_weight, fetched(down_weight),
    ]


def returned(own_here, own_left, own_right, near_here, near_left, near_right, far_here, far_left, far_right, two_up, two_down):
    n, d = own_here.shape
    h = d // 2
    two_up, two_down = shift(two_up, 1, 0), shift(two_down, -1, 0)
    far_up, far_down = two_up[:, d + h :], two_down[:, d + h :]
    far_right = jnp.concatenate([b16(far_right[:, :h] + f32(far_up)), b16(far_right[:, h:])], 1)
    far_left = jnp.concatenate([b16(far_left[:, :h]), b16(far_left[:, h:] + f32(far_down))], 1)
    far_p, far_m = shift(far_right, 1, 0), shift(far_left, -1, 0)
    near_right = jnp.concatenate([b16(near_right[:n] + f32(two_up[:, :d])), b16(near_right[n:])], 0)
    near_left = jnp.concatenate([b16(near_left[:n]), b16(near_left[n:] + f32(two_down[:, :d]))], 0)
    near_p, near_m = shift(near_right, 1, 0), shift(near_left, -1, 0)
    own_right = jnp.concatenate([b16(own_right[:, :h] + f32(two_up[:, d : d + h])), b16(own_right[:, h:])], 1)
    own_left = jnp.concatenate([b16(own_left[:, :h]), b16(own_left[:, h:] + f32(two_down[:, d : d + h]))], 1)
    own_right, own_left, far_p, far_m = lax.optimization_barrier((own_right, own_left, far_p, far_m))
    own_p, own_m = shift(own_right, 1, 0), shift(own_left, -1, 0)
    far_sum = b16(far_here + f32(far_p) + f32(far_m))
    by_above, by_below = shift(far_sum[:, :h], 0, 1), shift(far_sum[:, h:], 0, -1)
    near_sum = near_here + f32(near_p) + f32(near_m)
    below_sum, above_sum = near_sum[:n], near_sum[n:]
    above_sum = jnp.concatenate([b16(above_sum[:, :h] + f32(by_above)), b16(above_sum[:, h:])], 1)
    below_sum = jnp.concatenate([b16(below_sum[:, :h]), b16(below_sum[:, h:] + f32(by_below))], 1)
    from_below, from_above = shift(above_sum, 0, 1), shift(below_sum, 0, -1)
    return own_here + f32(own_p) + f32(own_m) + f32(from_below) + f32(from_above)


def on_device(tokens, norm_gain, gate_weight, up_weight, down_weight):
    own = rms_normed(tokens, norm_gain)
    terms = block_terms(gathered(own, gate_weight, up_weight, down_weight))
    return b16(f32(tokens) + returned(*terms))


def solution(mesh):
    return jax.shard_map(
        on_device,
        mesh=mesh,
        in_specs=(
            P(("dp", "tensor"), None),
            P(),
            P(None, "tensor"),
            P(None, "tensor"),
            P("tensor", None),
        ),
        out_specs=P(("dp", "tensor"), None),
        check_vma=False,
    )
```

```python
import jax
import jax.numpy as jnp
from jax import lax
from jax.experimental import pallas as pl
from jax.experimental.pallas import tpu as pltpu
from jax.sharding import PartitionSpec as P

SIDE = 4


def shift(block, dx, dz):
    pairs = [
        (x * SIDE + z, (x + dx) % SIDE * SIDE + (z + dz) % SIDE)
        for x in range(SIDE)
        for z in range(SIDE)
    ]
    return lax.ppermute(block, "tensor", pairs)


def b16(v):
    return v.astype(jnp.bfloat16)


def f32(v):
    return v.astype(jnp.float32)


def rms_normed(rows, gain):
    def kernel(rows_ref, gain_ref, out_ref):
        held = f32(rows_ref[...])
        scale = lax.rsqrt(jnp.mean(held * held, axis=1, keepdims=True) + 1e-05)
        out_ref[...] = b16(held * scale * gain_ref[...])

    vmem = pl.BlockSpec(memory_space=pltpu.VMEM)
    return pl.pallas_call(
        kernel,
        out_shape=pltpu.VMEM(rows.shape, jnp.bfloat16),
        in_specs=[vmem] * 2,
        out_specs=vmem,
        compiler_params=pltpu.CompilerParams(vmem_limit_bytes=4 * 1024 * 1024),
    )(*[pltpu.with_memory_space_constraint(v, pltpu.HBM) for v in (rows, gain.reshape(1, -1))])


def swiglu(n, *refs):
    ins, (gate_w, up_w, up_w2, down_w), outs, (rows, hidden) = refs[:15], refs[15:19], refs[19:-2], refs[-2:]
    plain, (two_up, two_down, below_2, above_2, far_2up, far_2down) = ins[:9], ins[9:]
    own_here, own_left, own_right, near_here, near_left, near_right, far_here, far_left, far_right = outs[:9]
    out_up, out_down = outs[9:]
    d = rows.shape[1]
    half = d // 2
    for ref, at in zip(plain, (0, 1, 2, 4, 5, 6, 8, 13, 14), strict=True):
        rows[at * n : at * n + ref.shape[0], :] = ref[...]
    rows[3 * n : 4 * n, :half] = two_up[:, d:]
    rows[3 * n : 4 * n, half:] = two_down[:, d:]
    rows[10 * n : 11 * n, :] = two_up[:, :d]
    rows[11 * n : 12 * n, :] = two_down[:, :d]
    rows[12 * n : 13 * n, :half] = below_2[...]
    rows[12 * n : 13 * n, half:] = above_2[...]
    rows[15 * n :, :half] = far_2up[...]
    rows[15 * n :, half:] = far_2down[...]

    def units(start, size):
        cut = pl.ds(start, size)
        gate = jnp.dot(rows[...], gate_w[:, cut], preferred_element_type=jnp.float32)
        up = jnp.dot(rows[:, :half], up_w[:, cut], preferred_element_type=jnp.float32)
        up = up + jnp.dot(rows[:, half:], up_w2[:, cut], preferred_element_type=jnp.float32)
        hidden[:, cut] = b16(gate / (1.0 + jnp.exp(-gate)) * up)

    step = 1024
    units(0, gate_w.shape[1])

    def columns(start, second):
        cut = pl.ds(start, step)
        terms = jnp.dot(hidden[...], down_w[:, cut], preferred_element_type=jnp.float32)

        def part(i, k=1):
            return terms[i * n : (i + k) * n]

        own_here[:, cut] = part(0)
        near_here[:, cut] = part(4, 2)
        far_here[:, cut] = part(12)
        near_left[:, cut] = part(6, 2)
        near_right[:, cut] = part(8, 2)
        own_left[:, cut] = part(1)
        own_right[:, cut] = part(2)
        far_left[:, cut] = part(13)
        far_right[:, cut] = part(14)
        out_up[:, cut] = b16(part(10))
        out_down[:, cut] = b16(part(11))
        if second:
            out_down[:, pl.ds(start + half, step)] = b16(part(3))
            out_down[:, pl.ds(start + d, step)] = b16(part(15))
        else:
            out_up[:, pl.ds(start + d, step)] = b16(part(3))
            out_up[:, pl.ds(start + d + half, step)] = b16(part(15))

    for second in (False, True):

        @pl.loop(0, half // step)
        def _(i):
            columns(pl.multiple_of(i * step, step) + second * half, second)


def block_terms(blocks):
    n, d = blocks[0].shape
    ff = blocks[-1].shape[0]
    b, f, h = jnp.bfloat16, jnp.float32, d // 2
    shapes = [
        (n, d, f), (n, d, f), (n, d, f), (2 * n, d, f), (2 * n, d, f), (2 * n, d, f),
        (n, d, f), (n, d, f), (n, d, f), (n, 2 * d, b), (n, 2 * d, b),
    ]
    vmem = pl.BlockSpec(memory_space=pltpu.VMEM)
    return pl.pallas_call(
        lambda *refs: swiglu(n, *refs),
        out_shape=[jax.ShapeDtypeStruct(s[:2], s[2]) for s in shapes],
        in_specs=[vmem] * len(blocks),
        out_specs=[vmem] * len(shapes),
        scratch_shapes=[pltpu.VMEM((16 * n, d), b), pltpu.VMEM((16 * n, ff), b)],
        compiler_params=pltpu.CompilerParams(vmem_limit_bytes=14 * 1024 * 1024),
        cost_estimate=pl.CostEstimate(flops=6 * 16 * n * d * ff, bytes_accessed=6 * d * ff, transcendentals=16 * n * ff),
    )(*[pltpu.with_memory_space_constraint(b, pltpu.VMEM) for b in blocks])


def fetched(weight, part=0, parts=1):
    size = weight.shape[0] // parts

    def kernel(source, target, done):
        copy = pltpu.make_async_copy(source.at[pl.ds(part * size, size), :], target, done)
        copy.start()
        copy.wait()

    return pl.pallas_call(
        kernel,
        out_shape=pltpu.VMEM((size, weight.shape[1]), weight.dtype),
        in_specs=[pl.BlockSpec(memory_space=pltpu.HBM)],
        out_specs=pl.BlockSpec(memory_space=pltpu.VMEM),
        scratch_shapes=[pltpu.SemaphoreType.DMA],
        compiler_params=pltpu.CompilerParams(vmem_limit_bytes=1024 * 1024),
        cost_estimate=pl.CostEstimate(flops=0, bytes_accessed=2 * size * weight.shape[1], transcendentals=0),
    )(pltpu.with_memory_space_constraint(weight, pltpu.HBM))


def gathered(own, gate_weight, up_weight, down_weight):
    n, d = own.shape
    h = d // 2
    below, above = lax.optimization_barrier((shift(own, 0, 1), shift(own, 0, -1)))
    own_l, own_r = shift(own, 1, 0), shift(own, -1, 0)
    near = jnp.concatenate([below, above], 0)
    gate_v, up_v = fetched(gate_weight), fetched(up_weight, 0, 2)
    near, own_l, own_r, gate_v, up_v, up_weight = lax.optimization_barrier((near, own_l, own_r, gate_v, up_v, up_weight))
    below_2, above_2 = shift(below[:, :h], 0, 1), shift(above[:, h:], 0, -1)
    near_l, near_r = lax.optimization_barrier((shift(near, 1, 0), shift(near, -1, 0)))
    far = jnp.concatenate([below_2, above_2], 1)
    far, up_v2 = lax.optimization_barrier((far, fetched(up_weight, 1, 2)))
    far_l, far_r = lax.optimization_barrier((shift(far, 1, 0), shift(far, -1, 0)))
    two_up = shift(jnp.concatenate([near_l[:n], own_l[:, :h]], 1), 1, 0)
    two_down = shift(jnp.concatenate([near_r[n:], own_r[:, h:]], 1), -1, 0)
    far_2up, far_2down = shift(far_l[:, :h], 1, 0), shift(far_r[:, h:], -1, 0)
    return [
        own, own_l, own_r, below, above, near_l, near_r, far_l, far_r,
        two_up, two_down, below_2, above_2, far_2up, far_2down, gate_v, up_v, up_v2, fetched(down_weight),
    ]


def returned(own_here, own_left, own_right, near_here, near_left, near_right, far_here, far_left, far_right, two_up, two_down):
    n, d = own_here.shape
    h = d // 2
    two_up, two_down = lax.optimization_barrier((shift(two_up, 1, 0), shift(two_down, -1, 0)))
    far_up, far_down = two_up[:, d + h :], two_down[:, d + h :]
    far_right = jnp.concatenate([b16(far_right[:, :h] + f32(far_up)), b16(far_right[:, h:])], 1)
    far_left = jnp.concatenate([b16(far_left[:, :h]), b16(far_left[:, h:] + f32(far_down))], 1)
    far_p, far_m = shift(far_right, 1, 0), shift(far_left, -1, 0)
    near_right = jnp.concatenate([b16(near_right[:n] + f32(two_up[:, :d])), b16(near_right[n:])], 0)
    near_left = jnp.concatenate([b16(near_left[:n]), b16(near_left[n:] + f32(two_down[:, :d]))], 0)
    near_p, near_m = shift(near_right, 1, 0), shift(near_left, -1, 0)
    far_sum = shift(b16(far_here + f32(far_p) + f32(far_m)), 0, 2)
    own_right = jnp.concatenate([b16(own_right[:, :h] + f32(two_up[:, d : d + h])), b16(own_right[:, h:])], 1)
    own_left = jnp.concatenate([b16(own_left[:, :h]), b16(own_left[:, h:] + f32(two_down[:, d : d + h]))], 1)
    own_right, own_left, near_p, near_m = lax.optimization_barrier((own_right, own_left, near_p, near_m))
    own_p, own_m = shift(own_right, 1, 0), shift(own_left, -1, 0)
    near_sum = b16(near_here + f32(near_p) + f32(near_m))
    from_below, from_above = shift(near_sum[n:], 0, 1), shift(near_sum[:n], 0, -1)
    return own_here + f32(own_p) + f32(own_m) + f32(far_sum) + f32(from_below) + f32(from_above)


def on_device(tokens, norm_gain, gate_weight, up_weight, down_weight):
    own = rms_normed(tokens, norm_gain)
    terms = block_terms(gathered(own, gate_weight, up_weight, down_weight))
    return b16(f32(tokens) + returned(*terms))


def solution(mesh):
    return jax.shard_map(
        on_device,
        mesh=mesh,
        in_specs=(
            P(("dp", "tensor"), None),
            P(),
            P(None, "tensor"),
            P(None, "tensor"),
            P("tensor", None),
        ),
        out_specs=P(("dp", "tensor"), None),
        check_vma=False,
    )
```

```python
import jax
import jax.numpy as jnp
from jax import lax
from jax.experimental import pallas as pl
from jax.experimental.pallas import tpu as pltpu
from jax.sharding import PartitionSpec as P

SIDE = 4


def shift(block, dx, dz):
    pairs = [
        (x * SIDE + z, (x + dx) % SIDE * SIDE + (z + dz) % SIDE)
        for x in range(SIDE)
        for z in range(SIDE)
    ]
    return lax.ppermute(block, "tensor", pairs)


def b16(v):
    return v.astype(jnp.bfloat16)


def f32(v):
    return v.astype(jnp.float32)


def rms_normed(rows, gain):
    def kernel(rows_ref, gain_ref, out_ref):
        held = f32(rows_ref[...])
        scale = lax.rsqrt(jnp.mean(held * held, axis=1, keepdims=True) + 1e-05)
        out_ref[...] = b16(held * scale * gain_ref[...])

    vmem = pl.BlockSpec(memory_space=pltpu.VMEM)
    return pl.pallas_call(
        kernel,
        out_shape=pltpu.VMEM(rows.shape, jnp.bfloat16),
        in_specs=[vmem] * 2,
        out_specs=vmem,
        compiler_params=pltpu.CompilerParams(vmem_limit_bytes=4 * 1024 * 1024),
    )(*[pltpu.with_memory_space_constraint(v, pltpu.HBM) for v in (rows, gain.reshape(1, -1))])


def placed(blocks):
    return [pltpu.with_memory_space_constraint(v, pltpu.VMEM) for v in blocks]


def hidden_of(rows, gate_w, up_w, up_w2):
    half = up_w.shape[0]
    gate = jnp.dot(rows[...], gate_w[...], preferred_element_type=jnp.float32)
    up = jnp.dot(rows[:, :half], up_w[...], preferred_element_type=jnp.float32)
    up = up + jnp.dot(rows[:, half:], up_w2[...], preferred_element_type=jnp.float32)
    return b16(gate / (1.0 + jnp.exp(-gate)) * up)


def early_hidden(own, own_l, own_r, own_2up, own_2down, below, above, far, weights):
    n, d = own.shape
    h, ff = d // 2, weights[0].shape[1]

    def kernel(own, own_l, own_r, own_2up, own_2down, below, above, far, gate_w, up_w, up_w2, out, rows):
        for i, ref in ((0, own), (1, own_l), (2, own_r), (4, below), (5, above), (6, far)):
            rows[i * n : (i + 1) * n, :] = ref[...]
        rows[3 * n : 4 * n, :h] = own_2up[...]
        rows[3 * n : 4 * n, h:] = own_2down[...]
        out[...] = hidden_of(rows, gate_w, up_w, up_w2)

    vmem = pl.BlockSpec(memory_space=pltpu.VMEM)
    return pl.pallas_call(
        kernel,
        out_shape=pltpu.VMEM((7 * n, ff), jnp.bfloat16),
        in_specs=[vmem] * 11,
        out_specs=vmem,
        scratch_shapes=[pltpu.VMEM((7 * n, d), jnp.bfloat16)],
        compiler_params=pltpu.CompilerParams(vmem_limit_bytes=8 * 1024 * 1024),
        cost_estimate=pl.CostEstimate(flops=4 * 7 * n * d * ff, bytes_accessed=0, transcendentals=7 * n * ff),
    )(*placed((own, own_l, own_r, own_2up, own_2down, below, above, far, *weights)))


def late_hidden(near_l, near_r, far_l, far_r, near_2up, near_2down, far_2up, far_2down, early, weights, down_weight):
    n, d = far_l.shape
    h, ff, step = d // 2, early.shape[1], 1024

    def kernel(
        near_l, near_r, far_l, far_r, near_2up, near_2down, far_2up, far_2down, early, gate_w, up_w, up_w2, source,
        out, out_up, out_down, down_w, rows, two, done,
    ):
        copy = pltpu.make_async_copy(source, down_w, done)
        copy.start()
        for i, ref in ((0, near_l), (2, near_r), (4, far_l), (5, far_r), (6, near_2up), (7, near_2down)):
            rows[i * n : i * n + ref.shape[0], :] = ref[...]
        rows[8 * n :, :h] = far_2up[...]
        rows[8 * n :, h:] = far_2down[...]
        out[...] = hidden_of(rows, gate_w, up_w, up_w2)
        two[:n, :] = early[3 * n : 4 * n, :]
        two[n:, :] = out[6 * n :, :]
        copy.wait()
        for second in (False, True):
            target = out_down if second else out_up

            @pl.loop(0, h // step)
            def _(i):
                start = pl.multiple_of(i * step, step)
                cut = pl.ds(start + second * h, step)
                terms = b16(jnp.dot(two[...], down_w[:, cut], preferred_element_type=jnp.float32))
                out_up[:, cut] = terms[n : 2 * n]
                out_down[:, cut] = terms[2 * n : 3 * n]
                target[:, pl.ds(start + d, step)] = terms[:n]
                target[:, pl.ds(start + d + h, step)] = terms[3 * n :]

    vmem, b = pl.BlockSpec(memory_space=pltpu.VMEM), jnp.bfloat16
    return pl.pallas_call(
        kernel,
        out_shape=[pltpu.VMEM(shape, b) for shape in ((9 * n, ff), (n, 2 * d), (n, 2 * d), (ff, d))],
        in_specs=[vmem] * 12 + [pl.BlockSpec(memory_space=pltpu.HBM)],
        out_specs=[vmem] * 4,
        scratch_shapes=[pltpu.VMEM((9 * n, d), b), pltpu.VMEM((4 * n, ff), b), pltpu.SemaphoreType.DMA],
        compiler_params=pltpu.CompilerParams(vmem_limit_bytes=10 * 1024 * 1024),
        cost_estimate=pl.CostEstimate(flops=4 * 11 * n * d * ff, bytes_accessed=2 * d * ff, transcendentals=9 * n * ff),
    )(
        *placed((near_l, near_r, far_l, far_r, near_2up, near_2down, far_2up, far_2down, early, *weights)),
        pltpu.with_memory_space_constraint(down_weight, pltpu.HBM),
    )


def other_terms(early, late, down_weight):
    n, (ff, d), step = early.shape[0] // 7, down_weight.shape, 1024
    tall = (1, 1, 1, 2, 1, 2, 2, 1, 1)

    def kernel(early, late, down_w, *rest):
        outs, held = rest[:-1], rest[-1]
        held[: 3 * n, :] = early[: 3 * n, :]
        held[3 * n : 6 * n, :] = early[4 * n :, :]
        held[6 * n :, :] = late[: 6 * n, :]

        @pl.loop(0, d // step)
        def _(i):
            cut = pl.ds(pl.multiple_of(i * step, step), step)
            terms = jnp.dot(held[...], down_w[:, cut], preferred_element_type=jnp.float32)
            at = 0
            for out, k in zip(outs, tall, strict=True):
                out[:, cut] = terms[at * n : (at + k) * n]
                at += k

    vmem = pl.BlockSpec(memory_space=pltpu.VMEM)
    return pl.pallas_call(
        kernel,
        out_shape=[pltpu.VMEM((k * n, d), jnp.float32) for k in tall],
        in_specs=[vmem] * 3,
        out_specs=[vmem] * 9,
        scratch_shapes=[pltpu.VMEM((12 * n, ff), jnp.bfloat16)],
        compiler_params=pltpu.CompilerParams(vmem_limit_bytes=8 * 1024 * 1024),
        cost_estimate=pl.CostEstimate(flops=2 * 12 * n * d * ff, bytes_accessed=0, transcendentals=0),
    )(*placed((early, late, down_weight)))


def fetched(weight, part=0, parts=1):
    size = weight.shape[0] // parts

    def kernel(source, target, done):
        copy = pltpu.make_async_copy(source.at[pl.ds(part * size, size), :], target, done)
        copy.start()
        copy.wait()

    return pl.pallas_call(
        kernel,
        out_shape=pltpu.VMEM((size, weight.shape[1]), weight.dtype),
        in_specs=[pl.BlockSpec(memory_space=pltpu.HBM)],
        out_specs=pl.BlockSpec(memory_space=pltpu.VMEM),
        scratch_shapes=[pltpu.SemaphoreType.DMA],
        compiler_params=pltpu.CompilerParams(vmem_limit_bytes=1024 * 1024),
        cost_estimate=pl.CostEstimate(flops=0, bytes_accessed=2 * size * weight.shape[1], transcendentals=0),
    )(pltpu.with_memory_space_constraint(weight, pltpu.HBM))


def terms_of(own, gate_weight, up_weight, down_weight):
    n, d = own.shape
    h = d // 2
    below, above = shift(own, 0, 1), shift(own, 0, -1)
    own_l, own_r, gate_v = lax.optimization_barrier((shift(own, 1, 0), shift(own, -1, 0), fetched(gate_weight)))
    own_2up, own_2down = shift(own_l[:, :h], 1, 0), shift(own_r[:, h:], -1, 0)
    below, above, own_2up, own_2down, up_v, up_weight = lax.optimization_barrier(
        (below, above, own_2up, own_2down, fetched(up_weight, 0, 2), up_weight)
    )
    near = jnp.concatenate([below, above], 0)
    below_2, above_2 = shift(below[:, :h], 0, 1), shift(above[:, h:], 0, -1)
    near_l, near_r = shift(near, 1, 0), shift(near, -1, 0)
    far, up_v2 = lax.optimization_barrier((jnp.concatenate([below_2, above_2], 1), fetched(up_weight, 1, 2)))
    weights = gate_v, up_v, up_v2
    early = early_hidden(own, own_l, own_r, own_2up, own_2down, below, above, far, weights)
    far_l, far_r = lax.optimization_barrier((shift(far, 1, 0), shift(far, -1, 0)))
    near_l, near_r, early = lax.optimization_barrier((near_l, near_r, early))
    near_2up, near_2down = shift(near_l[:n], 1, 0), shift(near_r[n:], -1, 0)
    far_2up, far_2down = shift(far_l[:, :h], 1, 0), shift(far_r[:, h:], -1, 0)
    late, two_up, two_down, down_v = late_hidden(
        near_l, near_r, far_l, far_r, near_2up, near_2down, far_2up, far_2down, early, weights, down_weight
    )
    return *other_terms(early, late, down_v), two_up, two_down


def returned(own_here, own_left, own_right, near_here, far_here, near_left, near_right, far_left, far_right, two_up, two_down):
    n, d = own_here.shape
    h = d // 2
    two_up, two_down = lax.optimization_barrier((shift(two_up, 1, 0), shift(two_down, -1, 0)))
    far_up, far_down = two_up[:, d + h :], two_down[:, d + h :]
    far_right = jnp.concatenate([b16(far_right[:, :h] + f32(far_up)), b16(far_right[:, h:])], 1)
    far_left = jnp.concatenate([b16(far_left[:, :h]), b16(far_left[:, h:] + f32(far_down))], 1)
    far_p, far_m = shift(far_right, 1, 0), shift(far_left, -1, 0)
    near_right = jnp.concatenate([b16(near_right[:n] + f32(two_up[:, :d])), b16(near_right[n:])], 0)
    near_left = jnp.concatenate([b16(near_left[:n]), b16(near_left[n:] + f32(two_down[:, :d]))], 0)
    near_p, near_m = shift(near_right, 1, 0), shift(near_left, -1, 0)
    far_sum = shift(b16(far_here + f32(far_p) + f32(far_m)), 0, 2)
    own_right = jnp.concatenate([b16(own_right[:, :h] + f32(two_up[:, d : d + h])), b16(own_right[:, h:])], 1)
    own_left = jnp.concatenate([b16(own_left[:, :h]), b16(own_left[:, h:] + f32(two_down[:, d : d + h]))], 1)
    own_right, own_left, near_p, near_m = lax.optimization_barrier((own_right, own_left, near_p, near_m))
    own_p, own_m = shift(own_right, 1, 0), shift(own_left, -1, 0)
    near_sum = b16(near_here + f32(near_p) + f32(near_m))
    from_below, from_above = shift(near_sum[n:], 0, 1), shift(near_sum[:n], 0, -1)
    return own_here + f32(own_p) + f32(own_m) + f32(far_sum) + f32(from_below) + f32(from_above)


def on_device(tokens, norm_gain, gate_weight, up_weight, down_weight):
    own = rms_normed(tokens, norm_gain)
    return b16(f32(tokens) + returned(*terms_of(own, gate_weight, up_weight, down_weight)))


def solution(mesh):
    return jax.shard_map(
        on_device,
        mesh=mesh,
        in_specs=(
            P(("dp", "tensor"), None),
            P(),
            P(None, "tensor"),
            P(None, "tensor"),
            P("tensor", None),
        ),
        out_specs=P(("dp", "tensor"), None),
        check_vma=False,
    )
```

```python
import jax
import jax.numpy as jnp
from jax import lax
from jax.experimental import pallas as pl
from jax.experimental.pallas import tpu as pltpu
from jax.sharding import PartitionSpec as P

SIDE = 4


def shift(block, dx, dz):
    pairs = [
        (x * SIDE + z, (x + dx) % SIDE * SIDE + (z + dz) % SIDE)
        for x in range(SIDE)
        for z in range(SIDE)
    ]
    return lax.ppermute(block, "tensor", pairs)


def b16(v):
    return v.astype(jnp.bfloat16)


def f32(v):
    return v.astype(jnp.float32)


def rms_normed(rows, gain):
    def kernel(rows_ref, gain_ref, out_ref):
        held = f32(rows_ref[...])
        scale = lax.rsqrt(jnp.mean(held * held, axis=1, keepdims=True) + 1e-05)
        out_ref[...] = b16(held * scale * gain_ref[...])

    vmem = pl.BlockSpec(memory_space=pltpu.VMEM)
    return pl.pallas_call(
        kernel,
        out_shape=pltpu.VMEM(rows.shape, jnp.bfloat16),
        in_specs=[vmem] * 2,
        out_specs=vmem,
        compiler_params=pltpu.CompilerParams(vmem_limit_bytes=4 * 1024 * 1024),
    )(*[pltpu.with_memory_space_constraint(v, pltpu.HBM) for v in (rows, gain.reshape(1, -1))])


def placed(blocks):
    return [pltpu.with_memory_space_constraint(v, pltpu.VMEM) for v in blocks]


def hidden_of(rows, gate_w, up_w, up_w2):
    half = up_w.shape[0]
    gate = jnp.dot(rows[...], gate_w[...], preferred_element_type=jnp.float32)
    up = jnp.dot(rows[:, :half], up_w[...], preferred_element_type=jnp.float32)
    up = up + jnp.dot(rows[:, half:], up_w2[...], preferred_element_type=jnp.float32)
    return b16(gate / (1.0 + jnp.exp(-gate)) * up)


def early_hidden(blocks, weights):
    (n, d), ff, sets = blocks[0].shape, weights[0].shape[1], len(blocks)

    def kernel(*refs):
        ins, ws, (out, rows) = refs[:sets], refs[sets:-2], refs[-2:]
        for i, ref in enumerate(ins):
            rows[i * n : (i + 1) * n, :] = ref[...]
        out[...] = hidden_of(rows, *ws)

    vmem = pl.BlockSpec(memory_space=pltpu.VMEM)
    return pl.pallas_call(
        kernel,
        out_shape=pltpu.VMEM((sets * n, ff), jnp.bfloat16),
        in_specs=[vmem] * (sets + len(weights)),
        out_specs=vmem,
        scratch_shapes=[pltpu.VMEM((sets * n, d), jnp.bfloat16)],
        compiler_params=pltpu.CompilerParams(vmem_limit_bytes=8 * 1024 * 1024),
        cost_estimate=pl.CostEstimate(flops=4 * sets * n * d * ff, bytes_accessed=0, transcendentals=sets * n * ff),
    )(*placed((*blocks, *weights)))


def late_hidden(near_l, near_r, far_l, far_r, two_up, two_down, far_2up, far_2down, weights, down_weight):
    n, d = far_l.shape
    (ff, _), h, step = down_weight.shape, d // 2, 1024

    def kernel(
        near_l, near_r, far_l, far_r, two_up, two_down, far_2up, far_2down, gate_w, up_w, up_w2, source,
        out, out_up, out_down, down_w, rows, done,
    ):
        copy = pltpu.make_async_copy(source, down_w, done)
        copy.start()
        for i, ref in ((0, near_l), (2, near_r), (4, far_l), (5, far_r)):
            rows[i * n : i * n + ref.shape[0], :] = ref[...]
        rows[6 * n : 7 * n, :] = two_up[:, :d]
        rows[7 * n : 8 * n, :] = two_down[:, :d]
        rows[8 * n : 9 * n, :h] = two_up[:, d:]
        rows[8 * n : 9 * n, h:] = two_down[:, d:]
        rows[9 * n :, :h] = far_2up[...]
        rows[9 * n :, h:] = far_2down[...]
        out[...] = hidden_of(rows, gate_w, up_w, up_w2)
        copy.wait()
        for second in (False, True):
            target = out_down if second else out_up

            @pl.loop(0, h // step)
            def _(i):
                start = pl.multiple_of(i * step, step)
                cut = pl.ds(start + second * h, step)
                terms = b16(jnp.dot(out[6 * n :, :], down_w[:, cut], preferred_element_type=jnp.float32))
                out_up[:, cut] = terms[:n]
                out_down[:, cut] = terms[n : 2 * n]
                target[:, pl.ds(start + d, step)] = terms[2 * n : 3 * n]
                target[:, pl.ds(start + d + h, step)] = terms[3 * n :]

    vmem, b = pl.BlockSpec(memory_space=pltpu.VMEM), jnp.bfloat16
    return pl.pallas_call(
        kernel,
        out_shape=[pltpu.VMEM(shape, b) for shape in ((10 * n, ff), (n, 2 * d), (n, 2 * d), (ff, d))],
        in_specs=[vmem] * 11 + [pl.BlockSpec(memory_space=pltpu.HBM)],
        out_specs=[vmem] * 4,
        scratch_shapes=[pltpu.VMEM((10 * n, d), b), pltpu.SemaphoreType.DMA],
        compiler_params=pltpu.CompilerParams(vmem_limit_bytes=10 * 1024 * 1024),
        cost_estimate=pl.CostEstimate(flops=4 * 12 * n * d * ff, bytes_accessed=2 * d * ff, transcendentals=10 * n * ff),
    )(
        *placed((near_l, near_r, far_l, far_r, two_up, two_down, far_2up, far_2down, *weights)),
        pltpu.with_memory_space_constraint(down_weight, pltpu.HBM),
    )


def other_terms(early, late, down_weight):
    n, (ff, d), step = early.shape[0] // 6, down_weight.shape, 1024
    tall = (1, 1, 1, 2, 1, 2, 2, 1, 1)

    def kernel(early, late, down_w, *rest):
        outs, held = rest[:-1], rest[-1]
        held[: 6 * n, :] = early[...]
        held[6 * n :, :] = late[: 6 * n, :]

        @pl.loop(0, d // step)
        def _(i):
            cut = pl.ds(pl.multiple_of(i * step, step), step)
            terms = jnp.dot(held[...], down_w[:, cut], preferred_element_type=jnp.float32)
            at = 0
            for out, k in zip(outs, tall, strict=True):
                out[:, cut] = terms[at * n : (at + k) * n]
                at += k

    vmem = pl.BlockSpec(memory_space=pltpu.VMEM)
    return pl.pallas_call(
        kernel,
        out_shape=[pltpu.VMEM((k * n, d), jnp.float32) for k in tall],
        in_specs=[vmem] * 3,
        out_specs=[vmem] * 9,
        scratch_shapes=[pltpu.VMEM((12 * n, ff), jnp.bfloat16)],
        compiler_params=pltpu.CompilerParams(vmem_limit_bytes=8 * 1024 * 1024),
        cost_estimate=pl.CostEstimate(flops=2 * 12 * n * d * ff, bytes_accessed=0, transcendentals=0),
    )(*placed((early, late, down_weight)))


def fetched(weight, part=0, parts=1):
    size = weight.shape[0] // parts

    def kernel(source, target, done):
        copy = pltpu.make_async_copy(source.at[pl.ds(part * size, size), :], target, done)
        copy.start()
        copy.wait()

    return pl.pallas_call(
        kernel,
        out_shape=pltpu.VMEM((size, weight.shape[1]), weight.dtype),
        in_specs=[pl.BlockSpec(memory_space=pltpu.HBM)],
        out_specs=pl.BlockSpec(memory_space=pltpu.VMEM),
        scratch_shapes=[pltpu.SemaphoreType.DMA],
        compiler_params=pltpu.CompilerParams(vmem_limit_bytes=1024 * 1024),
        cost_estimate=pl.CostEstimate(flops=0, bytes_accessed=2 * size * weight.shape[1], transcendentals=0),
    )(pltpu.with_memory_space_constraint(weight, pltpu.HBM))


def terms_of(own, gate_weight, up_weight, down_weight):
    n, d = own.shape
    h = d // 2
    below, above = lax.optimization_barrier((shift(own, 0, 1), shift(own, 0, -1)))
    own_l, own_r = shift(own, 1, 0), shift(own, -1, 0)
    below_2, above_2 = shift(below[:, :h], 0, 1), shift(above[:, h:], 0, -1)
    near, own_l, own_r, gate_v, up_v, up_weight = lax.optimization_barrier(
        (jnp.concatenate([below, above], 0), own_l, own_r, fetched(gate_weight), fetched(up_weight, 0, 2), up_weight)
    )
    near_l, near_r = shift(near, 1, 0), shift(near, -1, 0)
    far, up_v2 = lax.optimization_barrier((jnp.concatenate([below_2, above_2], 1), fetched(up_weight, 1, 2)))
    weights = gate_v, up_v, up_v2
    early = early_hidden((own, own_l, own_r, below, above, far), weights)
    far_l, far_r = lax.optimization_barrier((shift(far, 1, 0), shift(far, -1, 0)))
    near_l, near_r, early = lax.optimization_barrier((near_l, near_r, early))
    two_up = shift(jnp.concatenate([near_l[:n], own_l[:, :h]], 1), 1, 0)
    two_down = shift(jnp.concatenate([near_r[n:], own_r[:, h:]], 1), -1, 0)
    far_2up, far_2down = shift(far_l[:, :h], 1, 0), shift(far_r[:, h:], -1, 0)
    late, two_up, two_down, down_v = late_hidden(
        near_l, near_r, far_l, far_r, two_up, two_down, far_2up, far_2down, weights, down_weight
    )
    return *other_terms(early, late, down_v), two_up, two_down


def returned(own_here, own_left, own_right, near_here, far_here, near_left, near_right, far_left, far_right, two_up, two_down):
    n, d = own_here.shape
    h = d // 2
    two_up, two_down = lax.optimization_barrier((shift(two_up, 1, 0), shift(two_down, -1, 0)))
    far_up, far_down = two_up[:, d + h :], two_down[:, d + h :]
    far_right = jnp.concatenate([b16(far_right[:, :h] + f32(far_up)), b16(far_right[:, h:])], 1)
    far_left = jnp.concatenate([b16(far_left[:, :h]), b16(far_left[:, h:] + f32(far_down))], 1)
    far_p, far_m = shift(far_right, 1, 0), shift(far_left, -1, 0)
    near_right = jnp.concatenate([b16(near_right[:n] + f32(two_up[:, :d])), b16(near_right[n:])], 0)
    near_left = jnp.concatenate([b16(near_left[:n]), b16(near_left[n:] + f32(two_down[:, :d]))], 0)
    near_p, near_m = shift(near_right, 1, 0), shift(near_left, -1, 0)
    own_right = jnp.concatenate([b16(own_right[:, :h] + f32(two_up[:, d : d + h])), b16(own_right[:, h:])], 1)
    own_left = jnp.concatenate([b16(own_left[:, :h]), b16(own_left[:, h:] + f32(two_down[:, d : d + h]))], 1)
    own_right, own_left, near_p, near_m = lax.optimization_barrier((own_right, own_left, near_p, near_m))
    far_sum = shift(b16(far_here + f32(far_p) + f32(far_m)), 0, 2)
    own_p, own_m = shift(own_right, 1, 0), shift(own_left, -1, 0)
    near_sum = b16(near_here + f32(near_p) + f32(near_m))
    from_below, from_above = shift(near_sum[n:], 0, 1), shift(near_sum[:n], 0, -1)
    return own_here + f32(own_p) + f32(own_m) + f32(far_sum) + f32(from_below) + f32(from_above)


def on_device(tokens, norm_gain, gate_weight, up_weight, down_weight):
    own = rms_normed(tokens, norm_gain)
    return b16(f32(tokens) + returned(*terms_of(own, gate_weight, up_weight, down_weight)))


def solution(mesh):
    return jax.shard_map(
        on_device,
        mesh=mesh,
        in_specs=(
            P(("dp", "tensor"), None),
            P(),
            P(None, "tensor"),
            P(None, "tensor"),
            P("tensor", None),
        ),
        out_specs=P(("dp", "tensor"), None),
        check_vma=False,
    )
```

```python
import jax
import jax.numpy as jnp
from jax import lax
from jax.experimental import pallas as pl
from jax.experimental.pallas import tpu as pltpu
from jax.sharding import PartitionSpec as P

SIDE = 4


def shift(block, dx, dz):
    pairs = [
        (x * SIDE + z, (x + dx) % SIDE * SIDE + (z + dz) % SIDE)
        for x in range(SIDE)
        for z in range(SIDE)
    ]
    return lax.ppermute(block, "tensor", pairs)


def b16(v):
    return v.astype(jnp.bfloat16)


def f32(v):
    return v.astype(jnp.float32)


def rms_normed(rows, gain):
    def kernel(rows_ref, gain_ref, out_ref):
        held = f32(rows_ref[...])
        scale = lax.rsqrt(jnp.mean(held * held, axis=1, keepdims=True) + 1e-05)
        out_ref[...] = b16(held * scale * gain_ref[...])

    vmem = pl.BlockSpec(memory_space=pltpu.VMEM)
    return pl.pallas_call(
        kernel,
        out_shape=pltpu.VMEM(rows.shape, jnp.bfloat16),
        in_specs=[vmem] * 2,
        out_specs=vmem,
        compiler_params=pltpu.CompilerParams(vmem_limit_bytes=4 * 1024 * 1024),
    )(*[pltpu.with_memory_space_constraint(v, pltpu.HBM) for v in (rows, gain.reshape(1, -1))])


def placed(blocks):
    return [pltpu.with_memory_space_constraint(v, pltpu.VMEM) for v in blocks]


def hidden_of(rows, gate_w, up_w, up_w2):
    half = up_w.shape[0]
    gate = jnp.dot(rows[...], gate_w[...], preferred_element_type=jnp.float32)
    up = jnp.dot(rows[:, :half], up_w[...], preferred_element_type=jnp.float32)
    up = up + jnp.dot(rows[:, half:], up_w2[...], preferred_element_type=jnp.float32)
    return b16(gate / (1.0 + jnp.exp(-gate)) * up)


def hidden_units(blocks, weights, down_weight=None):
    (n, d), ff = blocks[0].shape, weights[0].shape[1]
    tall, held = sum(v.shape[0] for v in blocks), len(blocks)
    also = () if down_weight is None else (pltpu.with_memory_space_constraint(down_weight, pltpu.HBM),)

    def kernel(*refs):
        ins, ws, rest = refs[:held], refs[held : held + len(weights)], refs[held + len(weights) :]
        if also:
            source, out, target, rows, done = rest
            copy = pltpu.make_async_copy(source, target, done)
            copy.start()
        else:
            out, rows = rest
        at = 0
        for ref in ins:
            rows[at : at + ref.shape[0], :] = ref[...]
            at += ref.shape[0]
        out[...] = hidden_of(rows, *ws)
        if also:
            copy.wait()

    vmem, b = pl.BlockSpec(memory_space=pltpu.VMEM), jnp.bfloat16
    return pl.pallas_call(
        kernel,
        out_shape=[pltpu.VMEM((tall, ff), b)] + [pltpu.VMEM((ff, d), b) for _ in also],
        in_specs=[vmem] * (held + len(weights)) + [pl.BlockSpec(memory_space=pltpu.HBM) for _ in also],
        out_specs=[vmem] * (1 + len(also)),
        scratch_shapes=[pltpu.VMEM((tall, d), b)] + [pltpu.SemaphoreType.DMA for _ in also],
        compiler_params=pltpu.CompilerParams(vmem_limit_bytes=8 * 1024 * 1024),
        cost_estimate=pl.CostEstimate(flops=4 * tall * d * ff, bytes_accessed=2 * d * ff * len(also), transcendentals=tall * ff),
    )(*placed((*blocks, *weights)), *also)


def two_hops(two_up, two_down, far_up, far_down, weights, down_w):
    (n, h), (ff, d), step = far_up.shape, down_w.shape, 1024

    def kernel(two_up, two_down, far_up, far_down, gate_w, up_w, up_w2, down_w, out_up, out_down, rows, hidden):
        rows[:n, :] = two_up[:, :d]
        rows[n : 2 * n, :] = two_down[:, :d]
        rows[2 * n : 3 * n, :h] = two_up[:, d:]
        rows[2 * n : 3 * n, h:] = two_down[:, d:]
        rows[3 * n :, :h] = far_up[...]
        rows[3 * n :, h:] = far_down[...]
        hidden[...] = hidden_of(rows, gate_w, up_w, up_w2)
        for second in (False, True):
            target = out_down if second else out_up

            @pl.loop(0, h // step)
            def _(i):
                start = pl.multiple_of(i * step, step)
                cut = pl.ds(start + second * h, step)
                terms = b16(jnp.dot(hidden[...], down_w[:, cut], preferred_element_type=jnp.float32))
                out_up[:, cut] = terms[:n]
                out_down[:, cut] = terms[n : 2 * n]
                target[:, pl.ds(start + d, step)] = terms[2 * n : 3 * n]
                target[:, pl.ds(start + d + h, step)] = terms[3 * n :]

    vmem, b = pl.BlockSpec(memory_space=pltpu.VMEM), jnp.bfloat16
    return pl.pallas_call(
        kernel,
        out_shape=[pltpu.VMEM((n, 2 * d), b)] * 2,
        in_specs=[vmem] * 8,
        out_specs=[vmem] * 2,
        scratch_shapes=[pltpu.VMEM((4 * n, d), b), pltpu.VMEM((4 * n, ff), b)],
        compiler_params=pltpu.CompilerParams(vmem_limit_bytes=8 * 1024 * 1024),
        cost_estimate=pl.CostEstimate(flops=6 * 4 * n * d * ff, bytes_accessed=0, transcendentals=4 * n * ff),
    )(*placed((two_up, two_down, far_up, far_down, *weights, down_w)))


def other_terms(early, late, down_weight):
    n, (ff, d), step = early.shape[0] // 6, down_weight.shape, 1024
    tall = (1, 1, 1, 2, 1, 2, 2, 1, 1)

    def kernel(early, late, down_w, *rest):
        outs, held = rest[:-1], rest[-1]
        held[: 6 * n, :] = early[...]
        held[6 * n :, :] = late[...]

        @pl.loop(0, d // step)
        def _(i):
            cut = pl.ds(pl.multiple_of(i * step, step), step)
            terms = jnp.dot(held[...], down_w[:, cut], preferred_element_type=jnp.float32)
            at = 0
            for out, k in zip(outs, tall, strict=True):
                out[:, cut] = terms[at * n : (at + k) * n]
                at += k

    vmem = pl.BlockSpec(memory_space=pltpu.VMEM)
    return pl.pallas_call(
        kernel,
        out_shape=[pltpu.VMEM((k * n, d), jnp.float32) for k in tall],
        in_specs=[vmem] * 3,
        out_specs=[vmem] * 9,
        scratch_shapes=[pltpu.VMEM((12 * n, ff), jnp.bfloat16)],
        compiler_params=pltpu.CompilerParams(vmem_limit_bytes=8 * 1024 * 1024),
        cost_estimate=pl.CostEstimate(flops=2 * 12 * n * d * ff, bytes_accessed=0, transcendentals=0),
    )(*placed((early, late, down_weight)))


def fetched(weight, part=0, parts=1):
    size = weight.shape[0] // parts

    def kernel(source, target, done):
        copy = pltpu.make_async_copy(source.at[pl.ds(part * size, size), :], target, done)
        copy.start()
        copy.wait()

    return pl.pallas_call(
        kernel,
        out_shape=pltpu.VMEM((size, weight.shape[1]), weight.dtype),
        in_specs=[pl.BlockSpec(memory_space=pltpu.HBM)],
        out_specs=pl.BlockSpec(memory_space=pltpu.VMEM),
        scratch_shapes=[pltpu.SemaphoreType.DMA],
        compiler_params=pltpu.CompilerParams(vmem_limit_bytes=1024 * 1024),
        cost_estimate=pl.CostEstimate(flops=0, bytes_accessed=2 * size * weight.shape[1], transcendentals=0),
    )(pltpu.with_memory_space_constraint(weight, pltpu.HBM))


def terms_of(own, gate_weight, up_weight, down_weight):
    n, d = own.shape
    h = d // 2
    below, above = lax.optimization_barrier((shift(own, 0, 1), shift(own, 0, -1)))
    own_l, own_r = shift(own, 1, 0), shift(own, -1, 0)
    below_2, above_2 = shift(below[:, :h], 0, 1), shift(above[:, h:], 0, -1)
    near, own_l, own_r, gate_v, up_v, up_weight = lax.optimization_barrier(
        (jnp.concatenate([below, above], 0), own_l, own_r, fetched(gate_weight), fetched(up_weight, 0, 2), up_weight)
    )
    near_l, near_r = shift(near, 1, 0), shift(near, -1, 0)
    far, up_v2 = lax.optimization_barrier((jnp.concatenate([below_2, above_2], 1), fetched(up_weight, 1, 2)))
    weights = gate_v, up_v, up_v2
    (early,) = hidden_units((own, own_l, own_r, below, above, far), weights)
    far_l, far_r = lax.optimization_barrier((shift(far, 1, 0), shift(far, -1, 0)))
    near_l, near_r, early = lax.optimization_barrier((near_l, near_r, early))
    two_up = shift(jnp.concatenate([near_l[:n], own_l[:, :h]], 1), 1, 0)
    two_down = shift(jnp.concatenate([near_r[n:], own_r[:, h:]], 1), -1, 0)
    far_2up, far_2down = shift(far_l[:, :h], 1, 0), shift(far_r[:, h:], -1, 0)
    late, down_v = hidden_units((near_l, near_r, far_l, far_r), weights, down_weight)
    two_up, two_down = two_hops(two_up, two_down, far_2up, far_2down, weights, down_v)
    return *other_terms(early, late, down_v), two_up, two_down


def returned(own_here, own_left, own_right, near_here, far_here, near_left, near_right, far_left, far_right, two_up, two_down):
    n, d = own_here.shape
    h = d // 2
    two_up, two_down = lax.optimization_barrier((shift(two_up, 1, 0), shift(two_down, -1, 0)))
    far_up, far_down = two_up[:, d + h :], two_down[:, d + h :]
    far_right = jnp.concatenate([b16(far_right[:, :h] + f32(far_up)), b16(far_right[:, h:])], 1)
    far_left = jnp.concatenate([b16(far_left[:, :h]), b16(far_left[:, h:] + f32(far_down))], 1)
    far_p, far_m = shift(far_right, 1, 0), shift(far_left, -1, 0)
    near_right = jnp.concatenate([b16(near_right[:n] + f32(two_up[:, :d])), b16(near_right[n:])], 0)
    near_left = jnp.concatenate([b16(near_left[:n]), b16(near_left[n:] + f32(two_down[:, :d]))], 0)
    near_p, near_m = shift(near_right, 1, 0), shift(near_left, -1, 0)
    own_right = jnp.concatenate([b16(own_right[:, :h] + f32(two_up[:, d : d + h])), b16(own_right[:, h:])], 1)
    own_left = jnp.concatenate([b16(own_left[:, :h]), b16(own_left[:, h:] + f32(two_down[:, d : d + h]))], 1)
    own_right, own_left, near_p, near_m = lax.optimization_barrier((own_right, own_left, near_p, near_m))
    far_sum = shift(b16(far_here + f32(far_p) + f32(far_m)), 0, 2)
    own_p, own_m = shift(own_right, 1, 0), shift(own_left, -1, 0)
    near_sum = b16(near_here + f32(near_p) + f32(near_m))
    from_below, from_above = shift(near_sum[n:], 0, 1), shift(near_sum[:n], 0, -1)
    return own_here + f32(own_p) + f32(own_m) + f32(far_sum) + f32(from_below) + f32(from_above)


def on_device(tokens, norm_gain, gate_weight, up_weight, down_weight):
    own = rms_normed(tokens, norm_gain)
    return b16(f32(tokens) + returned(*terms_of(own, gate_weight, up_weight, down_weight)))


def solution(mesh):
    return jax.shard_map(
        on_device,
        mesh=mesh,
        in_specs=(
            P(("dp", "tensor"), None),
            P(),
            P(None, "tensor"),
            P(None, "tensor"),
            P("tensor", None),
        ),
        out_specs=P(("dp", "tensor"), None),
        check_vma=False,
    )
```

```python
import jax
import jax.numpy as jnp
from jax import lax
from jax.experimental import pallas as pl
from jax.experimental.pallas import tpu as pltpu
from jax.sharding import PartitionSpec as P

SIDE = 4


def shift(block, dx, dz):
    pairs = []
    for part in range(lax.axis_size("dp")):
        way = 1 - 2 * (part % 2)
        for x in range(SIDE):
            for z in range(SIDE):
                there = (x + way * dx) % SIDE * SIDE + (z + way * dz) % SIDE
                pairs.append((part * SIDE**2 + x * SIDE + z, part * SIDE**2 + there))
    return lax.ppermute(block, ("dp", "tensor"), pairs)


def b16(v):
    return v.astype(jnp.bfloat16)


def f32(v):
    return v.astype(jnp.float32)


def rms_normed(rows, gain):
    def kernel(rows_ref, gain_ref, out_ref):
        held = f32(rows_ref[...])
        scale = lax.rsqrt(jnp.mean(held * held, axis=1, keepdims=True) + 1e-05)
        out_ref[...] = b16(held * scale * gain_ref[...])

    vmem = pl.BlockSpec(memory_space=pltpu.VMEM)
    return pl.pallas_call(
        kernel,
        out_shape=pltpu.VMEM(rows.shape, jnp.bfloat16),
        in_specs=[vmem] * 2,
        out_specs=vmem,
        compiler_params=pltpu.CompilerParams(vmem_limit_bytes=4 * 1024 * 1024),
    )(*[pltpu.with_memory_space_constraint(v, pltpu.HBM) for v in (rows, gain.reshape(1, -1))])


def placed(blocks):
    return [pltpu.with_memory_space_constraint(v, pltpu.VMEM) for v in blocks]


def hidden_of(rows, gate_w, up_w, up_w2):
    half = up_w.shape[0]
    gate = jnp.dot(rows[...], gate_w[...], preferred_element_type=jnp.float32)
    up = jnp.dot(rows[:, :half], up_w[...], preferred_element_type=jnp.float32)
    up = up + jnp.dot(rows[:, half:], up_w2[...], preferred_element_type=jnp.float32)
    return b16(gate / (1.0 + jnp.exp(-gate)) * up)


def hidden_units(blocks, weights, down_weight=None):
    (n, d), ff = blocks[0].shape, weights[0].shape[1]
    tall, held = sum(v.shape[0] for v in blocks), len(blocks)
    also = () if down_weight is None else (pltpu.with_memory_space_constraint(down_weight, pltpu.HBM),)

    def kernel(*refs):
        ins, ws, rest = refs[:held], refs[held : held + len(weights)], refs[held + len(weights) :]
        if also:
            source, out, target, rows, done = rest
            copy = pltpu.make_async_copy(source, target, done)
            copy.start()
        else:
            out, rows = rest
        at = 0
        for ref in ins:
            rows[at : at + ref.shape[0], :] = ref[...]
            at += ref.shape[0]
        out[...] = hidden_of(rows, *ws)
        if also:
            copy.wait()

    vmem, b = pl.BlockSpec(memory_space=pltpu.VMEM), jnp.bfloat16
    return pl.pallas_call(
        kernel,
        out_shape=[pltpu.VMEM((tall, ff), b)] + [pltpu.VMEM((ff, d), b) for _ in also],
        in_specs=[vmem] * (held + len(weights)) + [pl.BlockSpec(memory_space=pltpu.HBM) for _ in also],
        out_specs=[vmem] * (1 + len(also)),
        scratch_shapes=[pltpu.VMEM((tall, d), b)] + [pltpu.SemaphoreType.DMA for _ in also],
        compiler_params=pltpu.CompilerParams(vmem_limit_bytes=8 * 1024 * 1024),
        cost_estimate=pl.CostEstimate(flops=4 * tall * d * ff, bytes_accessed=2 * d * ff * len(also), transcendentals=tall * ff),
    )(*placed((*blocks, *weights)), *also)


def two_hops(two, weights, down_w):
    rows, (ff, d), step = two.shape[0], down_w.shape, 1024

    def kernel(two, gate_w, up_w, up_w2, down_w, out, hidden):
        hidden[...] = hidden_of(two, gate_w, up_w, up_w2)

        @pl.loop(0, d // step)
        def _(i):
            cut = pl.ds(pl.multiple_of(i * step, step), step)
            out[:, cut] = b16(jnp.dot(hidden[...], down_w[:, cut], preferred_element_type=jnp.float32))

    vmem, b = pl.BlockSpec(memory_space=pltpu.VMEM), jnp.bfloat16
    return pl.pallas_call(
        kernel,
        out_shape=pltpu.VMEM((rows, d), b),
        in_specs=[vmem] * 5,
        out_specs=vmem,
        scratch_shapes=[pltpu.VMEM((rows, ff), b)],
        compiler_params=pltpu.CompilerParams(vmem_limit_bytes=8 * 1024 * 1024),
        cost_estimate=pl.CostEstimate(flops=6 * rows * d * ff, bytes_accessed=0, transcendentals=rows * ff),
    )(*placed((two, *weights, down_w)))


def other_terms(early, late, down_weight):
    n, (ff, d), step = early.shape[0] // 6, down_weight.shape, 1024
    b, f = jnp.bfloat16, jnp.float32
    made = ((1, f), (1, f), (1, b), (2, f), (1, f), (2, f), (2, b), (1, f), (1, b))

    def kernel(early, late, down_w, *rest):
        outs, held = rest[:-1], rest[-1]
        held[: 6 * n, :] = early[...]
        held[6 * n :, :] = late[...]

        @pl.loop(0, d // step)
        def _(i):
            cut = pl.ds(pl.multiple_of(i * step, step), step)
            terms = jnp.dot(held[...], down_w[:, cut], preferred_element_type=jnp.float32)
            at = 0
            for out, (k, kind) in zip(outs, made, strict=True):
                out[:, cut] = terms[at * n : (at + k) * n].astype(kind)
                at += k

    vmem = pl.BlockSpec(memory_space=pltpu.VMEM)
    return pl.pallas_call(
        kernel,
        out_shape=[pltpu.VMEM((k * n, d), kind) for k, kind in made],
        in_specs=[vmem] * 3,
        out_specs=[vmem] * 9,
        scratch_shapes=[pltpu.VMEM((12 * n, ff), jnp.bfloat16)],
        compiler_params=pltpu.CompilerParams(vmem_limit_bytes=8 * 1024 * 1024),
        cost_estimate=pl.CostEstimate(flops=2 * 12 * n * d * ff, bytes_accessed=0, transcendentals=0),
    )(*placed((early, late, down_weight)))


def fetched(weight, part=0, parts=1):
    size = weight.shape[0] // parts

    def kernel(source, target, done):
        copy = pltpu.make_async_copy(source.at[pl.ds(part * size, size), :], target, done)
        copy.start()
        copy.wait()

    return pl.pallas_call(
        kernel,
        out_shape=pltpu.VMEM((size, weight.shape[1]), weight.dtype),
        in_specs=[pl.BlockSpec(memory_space=pltpu.HBM)],
        out_specs=pl.BlockSpec(memory_space=pltpu.VMEM),
        scratch_shapes=[pltpu.SemaphoreType.DMA],
        compiler_params=pltpu.CompilerParams(vmem_limit_bytes=1024 * 1024),
        cost_estimate=pl.CostEstimate(flops=0, bytes_accessed=2 * size * weight.shape[1], transcendentals=0),
    )(pltpu.with_memory_space_constraint(weight, pltpu.HBM))


def terms_of(own, gate_weight, up_weight, down_weight):
    below, above = lax.optimization_barrier((shift(own, 0, 1), shift(own, 0, -1)))
    own_p, own_m = shift(own, 1, 0), shift(own, -1, 0)
    far = shift(below, 0, 1)
    near, own_p, own_m, gate_v, up_v, up_weight = lax.optimization_barrier(
        (jnp.concatenate([below, above], 0), own_p, own_m, fetched(gate_weight), fetched(up_weight, 0, 2), up_weight)
    )
    near_p, near_m = shift(near, 1, 0), shift(near, -1, 0)
    far, up_v2 = lax.optimization_barrier((far, fetched(up_weight, 1, 2)))
    weights = gate_v, up_v, up_v2
    (early,) = hidden_units((own, own_p, own_m, below, above, far), weights)
    far_p, far_m = shift(far, 1, 0), shift(far, -1, 0)
    near_p, near_m, far_p, far_m, early = lax.optimization_barrier((near_p, near_m, far_p, far_m, early))
    two = shift(jnp.concatenate([near_p, own_p, far_p], 0), 1, 0)
    late, down_v = hidden_units((near_p, near_m, far_p, far_m), weights, down_weight)
    back = two_hops(two, weights, down_v)
    return *other_terms(early, late, down_v), back


def returned(own_here, own_p, own_m, near_here, far_here, near_p, near_m, far_p, far_m, two):
    n = own_here.shape[0]
    two = shift(two, -1, 0)
    far_m, near_m = shift(far_m, 1, 0), shift(near_m, 1, 0)
    far_p = shift(b16(far_p + f32(two[3 * n :])), -1, 0)
    near_p = shift(b16(near_p + f32(two[: 2 * n])), -1, 0)
    far_sum = shift(b16(far_here + f32(far_p) + f32(far_m)), 0, 2)
    own_p, own_m, near_p, near_m = lax.optimization_barrier((b16(own_p + f32(two[2 * n : 3 * n])), own_m, near_p, near_m))
    own_p, own_m = shift(own_p, -1, 0), shift(own_m, 1, 0)
    near_sum = b16(near_here + f32(near_p) + f32(near_m))
    from_above, from_below = shift(near_sum[:n], 0, -1), shift(near_sum[n:], 0, 1)
    return own_here + f32(own_p) + f32(own_m) + f32(far_sum) + f32(from_below) + f32(from_above)


def on_device(tokens, norm_gain, gate_weight, up_weight, down_weight):
    own = rms_normed(tokens, norm_gain)
    return b16(f32(tokens) + returned(*terms_of(own, gate_weight, up_weight, down_weight)))


def solution(mesh):
    return jax.shard_map(
        on_device,
        mesh=mesh,
        in_specs=(
            P(("dp", "tensor"), None),
            P(),
            P(None, "tensor"),
            P(None, "tensor"),
            P("tensor", None),
        ),
        out_specs=P(("dp", "tensor"), None),
        check_vma=False,
    )
```

```python
import jax
import jax.numpy as jnp
from jax import lax
from jax.experimental import pallas as pl
from jax.experimental.pallas import tpu as pltpu
from jax.sharding import PartitionSpec as P

SIDE = 4


def shift(block, dx, dz):
    pairs = []
    for part in range(lax.axis_size("dp")):
        way = 1 - 2 * (part % 2)
        for x in range(SIDE):
            for z in range(SIDE):
                there = (x + dx) % SIDE * SIDE + (z + way * dz) % SIDE
                pairs.append((part * SIDE**2 + x * SIDE + z, part * SIDE**2 + there))
    return lax.ppermute(block, ("dp", "tensor"), pairs)


def b16(v):
    return v.astype(jnp.bfloat16)


def f32(v):
    return v.astype(jnp.float32)


def rms_normed(rows, gain):
    def kernel(rows_ref, gain_ref, out_ref):
        held = f32(rows_ref[...])
        scale = lax.rsqrt(jnp.mean(held * held, axis=1, keepdims=True) + 1e-05)
        out_ref[...] = b16(held * scale * gain_ref[...])

    vmem = pl.BlockSpec(memory_space=pltpu.VMEM)
    return pl.pallas_call(
        kernel,
        out_shape=pltpu.VMEM(rows.shape, jnp.bfloat16),
        in_specs=[vmem] * 2,
        out_specs=vmem,
        compiler_params=pltpu.CompilerParams(vmem_limit_bytes=4 * 1024 * 1024),
    )(*[pltpu.with_memory_space_constraint(v, pltpu.HBM) for v in (rows, gain.reshape(1, -1))])


def placed(blocks):
    return [pltpu.with_memory_space_constraint(v, pltpu.VMEM) for v in blocks]


def hidden_of(rows, gate_w, up_w, up_w2):
    half = up_w.shape[0]
    gate = jnp.dot(rows[...], gate_w[...], preferred_element_type=jnp.float32)
    up = jnp.dot(rows[:, :half], up_w[...], preferred_element_type=jnp.float32)
    up = up + jnp.dot(rows[:, half:], up_w2[...], preferred_element_type=jnp.float32)
    return b16(gate / (1.0 + jnp.exp(-gate)) * up)


def hidden_units(blocks, weights, down_weight=None):
    (n, d), ff = blocks[0].shape, weights[0].shape[1]
    tall, held = sum(v.shape[0] for v in blocks), len(blocks)
    also = () if down_weight is None else (pltpu.with_memory_space_constraint(down_weight, pltpu.HBM),)

    def kernel(*refs):
        ins, ws, rest = refs[:held], refs[held : held + len(weights)], refs[held + len(weights) :]
        if also:
            source, out, target, rows, done = rest
            copy = pltpu.make_async_copy(source, target, done)
            copy.start()
        else:
            out, rows = rest
        at = 0
        for ref in ins:
            rows[at : at + ref.shape[0], :] = ref[...]
            at += ref.shape[0]
        out[...] = hidden_of(rows, *ws)
        if also:
            copy.wait()

    vmem, b = pl.BlockSpec(memory_space=pltpu.VMEM), jnp.bfloat16
    return pl.pallas_call(
        kernel,
        out_shape=[pltpu.VMEM((tall, ff), b)] + [pltpu.VMEM((ff, d), b) for _ in also],
        in_specs=[vmem] * (held + len(weights)) + [pl.BlockSpec(memory_space=pltpu.HBM) for _ in also],
        out_specs=[vmem] * (1 + len(also)),
        scratch_shapes=[pltpu.VMEM((tall, d), b)] + [pltpu.SemaphoreType.DMA for _ in also],
        compiler_params=pltpu.CompilerParams(vmem_limit_bytes=8 * 1024 * 1024),
        cost_estimate=pl.CostEstimate(flops=4 * tall * d * ff, bytes_accessed=2 * d * ff * len(also), transcendentals=tall * ff),
    )(*placed((*blocks, *weights)), *also)


def two_hops(two_up, two_down, far_up, far_down, weights, down_w):
    (n, h), (ff, d), step = far_up.shape, down_w.shape, 1024

    def kernel(two_up, two_down, far_up, far_down, gate_w, up_w, up_w2, down_w, out_up, out_down, rows, hidden):
        rows[:n, :] = two_up[:, :d]
        rows[n : 2 * n, :] = two_down[:, :d]
        rows[2 * n : 3 * n, :h] = two_up[:, d:]
        rows[2 * n : 3 * n, h:] = two_down[:, d:]
        rows[3 * n :, :h] = far_up[...]
        rows[3 * n :, h:] = far_down[...]
        hidden[...] = hidden_of(rows, gate_w, up_w, up_w2)
        for second in (False, True):
            target = out_down if second else out_up

            @pl.loop(0, h // step)
            def _(i):
                start = pl.multiple_of(i * step, step)
                cut = pl.ds(start + second * h, step)
                terms = b16(jnp.dot(hidden[...], down_w[:, cut], preferred_element_type=jnp.float32))
                out_up[:, cut] = terms[:n]
                out_down[:, cut] = terms[n : 2 * n]
                target[:, pl.ds(start + d, step)] = terms[2 * n : 3 * n]
                target[:, pl.ds(start + d + h, step)] = terms[3 * n :]

    vmem, b = pl.BlockSpec(memory_space=pltpu.VMEM), jnp.bfloat16
    return pl.pallas_call(
        kernel,
        out_shape=[pltpu.VMEM((n, 2 * d), b)] * 2,
        in_specs=[vmem] * 8,
        out_specs=[vmem] * 2,
        scratch_shapes=[pltpu.VMEM((4 * n, d), b), pltpu.VMEM((4 * n, ff), b)],
        compiler_params=pltpu.CompilerParams(vmem_limit_bytes=8 * 1024 * 1024),
        cost_estimate=pl.CostEstimate(flops=6 * 4 * n * d * ff, bytes_accessed=0, transcendentals=4 * n * ff),
    )(*placed((two_up, two_down, far_up, far_down, *weights, down_w)))


def other_terms(early, late, down_weight):
    n, (ff, d), step = early.shape[0] // 6, down_weight.shape, 1024
    tall = (1, 1, 1, 2, 1, 2, 2, 1, 1)

    def kernel(early, late, down_w, *rest):
        outs, held = rest[:-1], rest[-1]
        held[: 6 * n, :] = early[...]
        held[6 * n :, :] = late[...]

        @pl.loop(0, d // step)
        def _(i):
            cut = pl.ds(pl.multiple_of(i * step, step), step)
            terms = jnp.dot(held[...], down_w[:, cut], preferred_element_type=jnp.float32)
            at = 0
            for out, k in zip(outs, tall, strict=True):
                out[:, cut] = terms[at * n : (at + k) * n]
                at += k

    vmem = pl.BlockSpec(memory_space=pltpu.VMEM)
    return pl.pallas_call(
        kernel,
        out_shape=[pltpu.VMEM((k * n, d), jnp.float32) for k in tall],
        in_specs=[vmem] * 3,
        out_specs=[vmem] * 9,
        scratch_shapes=[pltpu.VMEM((12 * n, ff), jnp.bfloat16)],
        compiler_params=pltpu.CompilerParams(vmem_limit_bytes=8 * 1024 * 1024),
        cost_estimate=pl.CostEstimate(flops=2 * 12 * n * d * ff, bytes_accessed=0, transcendentals=0),
    )(*placed((early, late, down_weight)))


def fetched(weight, part=0, parts=1):
    size = weight.shape[0] // parts

    def kernel(source, target, done):
        copy = pltpu.make_async_copy(source.at[pl.ds(part * size, size), :], target, done)
        copy.start()
        copy.wait()

    return pl.pallas_call(
        kernel,
        out_shape=pltpu.VMEM((size, weight.shape[1]), weight.dtype),
        in_specs=[pl.BlockSpec(memory_space=pltpu.HBM)],
        out_specs=pl.BlockSpec(memory_space=pltpu.VMEM),
        scratch_shapes=[pltpu.SemaphoreType.DMA],
        compiler_params=pltpu.CompilerParams(vmem_limit_bytes=1024 * 1024),
        cost_estimate=pl.CostEstimate(flops=0, bytes_accessed=2 * size * weight.shape[1], transcendentals=0),
    )(pltpu.with_memory_space_constraint(weight, pltpu.HBM))


def terms_of(own, gate_weight, up_weight, down_weight):
    n, d = own.shape
    h = d // 2
    below, above = lax.optimization_barrier((shift(own, 0, 1), shift(own, 0, -1)))
    own_l, own_r = shift(own, 1, 0), shift(own, -1, 0)
    far = shift(below, 0, 1)
    near, own_l, own_r, gate_v, up_v, up_weight = lax.optimization_barrier(
        (jnp.concatenate([below, above], 0), own_l, own_r, fetched(gate_weight), fetched(up_weight, 0, 2), up_weight)
    )
    near_l, near_r = shift(near, 1, 0), shift(near, -1, 0)
    far, up_v2 = lax.optimization_barrier((far, fetched(up_weight, 1, 2)))
    weights = gate_v, up_v, up_v2
    (early,) = hidden_units((own, own_l, own_r, below, above, far), weights)
    far_l, far_r = lax.optimization_barrier((shift(far, 1, 0), shift(far, -1, 0)))
    near_l, near_r, early = lax.optimization_barrier((near_l, near_r, early))
    two_up = shift(jnp.concatenate([near_l[:n], own_l[:, :h]], 1), 1, 0)
    two_down = shift(jnp.concatenate([near_r[n:], own_r[:, h:]], 1), -1, 0)
    far_2up, far_2down = shift(far_l[:, :h], 1, 0), shift(far_r[:, h:], -1, 0)
    late, down_v = hidden_units((near_l, near_r, far_l, far_r), weights, down_weight)
    two_up, two_down = two_hops(two_up, two_down, far_2up, far_2down, weights, down_v)
    return *other_terms(early, late, down_v), two_up, two_down


def returned(own_here, own_left, own_right, near_here, far_here, near_left, near_right, far_left, far_right, two_up, two_down):
    n, d = own_here.shape
    h = d // 2
    two_up, two_down = lax.optimization_barrier((shift(two_up, 1, 0), shift(two_down, -1, 0)))
    far_up, far_down = two_up[:, d + h :], two_down[:, d + h :]
    far_right = jnp.concatenate([b16(far_right[:, :h] + f32(far_up)), b16(far_right[:, h:])], 1)
    far_left = jnp.concatenate([b16(far_left[:, :h]), b16(far_left[:, h:] + f32(far_down))], 1)
    far_p, far_m = shift(far_right, 1, 0), shift(far_left, -1, 0)
    near_right = jnp.concatenate([b16(near_right[:n] + f32(two_up[:, :d])), b16(near_right[n:])], 0)
    near_left = jnp.concatenate([b16(near_left[:n]), b16(near_left[n:] + f32(two_down[:, :d]))], 0)
    near_p, near_m = shift(near_right, 1, 0), shift(near_left, -1, 0)
    own_right = jnp.concatenate([b16(own_right[:, :h] + f32(two_up[:, d : d + h])), b16(own_right[:, h:])], 1)
    own_left = jnp.concatenate([b16(own_left[:, :h]), b16(own_left[:, h:] + f32(two_down[:, d : d + h]))], 1)
    own_right, own_left, near_p, near_m = lax.optimization_barrier((own_right, own_left, near_p, near_m))
    far_sum = shift(b16(far_here + f32(far_p) + f32(far_m)), 0, 2)
    own_p, own_m = shift(own_right, 1, 0), shift(own_left, -1, 0)
    near_sum = b16(near_here + f32(near_p) + f32(near_m))
    from_below, from_above = shift(near_sum[n:], 0, 1), shift(near_sum[:n], 0, -1)
    return own_here + f32(own_p) + f32(own_m) + f32(far_sum) + f32(from_below) + f32(from_above)


def on_device(tokens, norm_gain, gate_weight, up_weight, down_weight):
    own = rms_normed(tokens, norm_gain)
    return b16(f32(tokens) + returned(*terms_of(own, gate_weight, up_weight, down_weight)))


def solution(mesh):
    return jax.shard_map(
        on_device,
        mesh=mesh,
        in_specs=(
            P(("dp", "tensor"), None),
            P(),
            P(None, "tensor"),
            P(None, "tensor"),
            P("tensor", None),
        ),
        out_specs=P(("dp", "tensor"), None),
        check_vma=False,
    )
```

```python
import jax
import jax.numpy as jnp
from jax import lax
from jax.experimental import pallas as pl
from jax.experimental.pallas import tpu as pltpu
from jax.sharding import PartitionSpec as P

SIDE = 4


def shift(block, dx, dz):
    pairs = []
    for part in range(lax.axis_size("dp")):
        way = 1 - 2 * (part % 2)
        for x in range(SIDE):
            for z in range(SIDE):
                there = (x + dx) % SIDE * SIDE + (z + way * dz) % SIDE
                pairs.append((part * SIDE**2 + x * SIDE + z, part * SIDE**2 + there))
    return lax.ppermute(block, ("dp", "tensor"), pairs)


def b16(v):
    return v.astype(jnp.bfloat16)


def f32(v):
    return v.astype(jnp.float32)


def rms_normed(rows, gain):
    def kernel(rows_ref, gain_ref, out_ref):
        held = f32(rows_ref[...])
        scale = lax.rsqrt(jnp.mean(held * held, axis=1, keepdims=True) + 1e-05)
        out_ref[...] = b16(held * scale * gain_ref[...])

    vmem = pl.BlockSpec(memory_space=pltpu.VMEM)
    return pl.pallas_call(
        kernel,
        out_shape=pltpu.VMEM(rows.shape, jnp.bfloat16),
        in_specs=[vmem] * 2,
        out_specs=vmem,
        compiler_params=pltpu.CompilerParams(vmem_limit_bytes=4 * 1024 * 1024),
    )(*[pltpu.with_memory_space_constraint(v, pltpu.HBM) for v in (rows, gain.reshape(1, -1))])


def placed(blocks):
    return [pltpu.with_memory_space_constraint(v, pltpu.VMEM) for v in blocks]


def hidden_of(rows, gate_w, up_w, up_w2):
    half = up_w.shape[0]
    gate = jnp.dot(rows[...], gate_w[...], preferred_element_type=jnp.float32)
    up = jnp.dot(rows[:, :half], up_w[...], preferred_element_type=jnp.float32)
    up = up + jnp.dot(rows[:, half:], up_w2[...], preferred_element_type=jnp.float32)
    return b16(gate / (1.0 + jnp.exp(-gate)) * up)


def hidden_units(blocks, weights, down_weight=None):
    (n, d), ff = blocks[0].shape, weights[0].shape[1]
    tall, held = sum(v.shape[0] for v in blocks), len(blocks)
    also = () if down_weight is None else (pltpu.with_memory_space_constraint(down_weight, pltpu.HBM),)

    def kernel(*refs):
        ins, ws, rest = refs[:held], refs[held : held + len(weights)], refs[held + len(weights) :]
        if also:
            source, out, target, rows, done = rest
            copy = pltpu.make_async_copy(source, target, done)
            copy.start()
        else:
            out, rows = rest
        at = 0
        for ref in ins:
            rows[at : at + ref.shape[0], :] = ref[...]
            at += ref.shape[0]
        out[...] = hidden_of(rows, *ws)
        if also:
            copy.wait()

    vmem, b = pl.BlockSpec(memory_space=pltpu.VMEM), jnp.bfloat16
    return pl.pallas_call(
        kernel,
        out_shape=[pltpu.VMEM((tall, ff), b)] + [pltpu.VMEM((ff, d), b) for _ in also],
        in_specs=[vmem] * (held + len(weights)) + [pl.BlockSpec(memory_space=pltpu.HBM) for _ in also],
        out_specs=[vmem] * (1 + len(also)),
        scratch_shapes=[pltpu.VMEM((tall, d), b)] + [pltpu.SemaphoreType.DMA for _ in also],
        compiler_params=pltpu.CompilerParams(vmem_limit_bytes=8 * 1024 * 1024),
        cost_estimate=pl.CostEstimate(flops=4 * tall * d * ff, bytes_accessed=2 * d * ff * len(also), transcendentals=tall * ff),
    )(*placed((*blocks, *weights)), *also)


def two_hops(two_up, two_down, far_up, far_down, weights, down_w):
    (n, h), (ff, d), step = far_up.shape, down_w.shape, 1024

    def kernel(two_up, two_down, far_up, far_down, gate_w, up_w, up_w2, down_w, out_up, out_down, rows, hidden):
        rows[:n, :] = two_up[:, :d]
        rows[n : 2 * n, :] = two_down[:, :d]
        rows[2 * n : 3 * n, :h] = two_up[:, d:]
        rows[2 * n : 3 * n, h:] = two_down[:, d:]
        rows[3 * n :, :h] = far_up[...]
        rows[3 * n :, h:] = far_down[...]
        hidden[...] = hidden_of(rows, gate_w, up_w, up_w2)
        for second in (False, True):
            target = out_down if second else out_up

            @pl.loop(0, h // step)
            def _(i):
                start = pl.multiple_of(i * step, step)
                cut = pl.ds(start + second * h, step)
                terms = b16(jnp.dot(hidden[...], down_w[:, cut], preferred_element_type=jnp.float32))
                out_up[:, cut] = terms[:n]
                out_down[:, cut] = terms[n : 2 * n]
                target[:, pl.ds(start + d, step)] = terms[2 * n : 3 * n]
                target[:, pl.ds(start + d + h, step)] = terms[3 * n :]

    vmem, b = pl.BlockSpec(memory_space=pltpu.VMEM), jnp.bfloat16
    return pl.pallas_call(
        kernel,
        out_shape=[pltpu.VMEM((n, 2 * d), b)] * 2,
        in_specs=[vmem] * 8,
        out_specs=[vmem] * 2,
        scratch_shapes=[pltpu.VMEM((4 * n, d), b), pltpu.VMEM((4 * n, ff), b)],
        compiler_params=pltpu.CompilerParams(vmem_limit_bytes=8 * 1024 * 1024),
        cost_estimate=pl.CostEstimate(flops=6 * 4 * n * d * ff, bytes_accessed=0, transcendentals=4 * n * ff),
    )(*placed((two_up, two_down, far_up, far_down, *weights, down_w)))


def other_terms(early, late, down_weight):
    n, (ff, d), step = early.shape[0] // 6, down_weight.shape, 1024
    tall = (1, 1, 1, 2, 1, 2, 2, 1, 1)

    def kernel(early, late, down_w, *rest):
        outs, held = rest[:-1], rest[-1]
        held[: 6 * n, :] = early[...]
        held[6 * n :, :] = late[...]

        @pl.loop(0, d // step)
        def _(i):
            cut = pl.ds(pl.multiple_of(i * step, step), step)
            terms = jnp.dot(held[...], down_w[:, cut], preferred_element_type=jnp.float32)
            at = 0
            for out, k in zip(outs, tall, strict=True):
                out[:, cut] = terms[at * n : (at + k) * n]
                at += k

    vmem = pl.BlockSpec(memory_space=pltpu.VMEM)
    return pl.pallas_call(
        kernel,
        out_shape=[pltpu.VMEM((k * n, d), jnp.float32) for k in tall],
        in_specs=[vmem] * 3,
        out_specs=[vmem] * 9,
        scratch_shapes=[pltpu.VMEM((12 * n, ff), jnp.bfloat16)],
        compiler_params=pltpu.CompilerParams(vmem_limit_bytes=8 * 1024 * 1024),
        cost_estimate=pl.CostEstimate(flops=2 * 12 * n * d * ff, bytes_accessed=0, transcendentals=0),
    )(*placed((early, late, down_weight)))


def fetched(weight, part=0, parts=1):
    size = weight.shape[0] // parts

    def kernel(source, target, done):
        copy = pltpu.make_async_copy(source.at[pl.ds(part * size, size), :], target, done)
        copy.start()
        copy.wait()

    return pl.pallas_call(
        kernel,
        out_shape=pltpu.VMEM((size, weight.shape[1]), weight.dtype),
        in_specs=[pl.BlockSpec(memory_space=pltpu.HBM)],
        out_specs=pl.BlockSpec(memory_space=pltpu.VMEM),
        scratch_shapes=[pltpu.SemaphoreType.DMA],
        compiler_params=pltpu.CompilerParams(vmem_limit_bytes=1024 * 1024),
        cost_estimate=pl.CostEstimate(flops=0, bytes_accessed=2 * size * weight.shape[1], transcendentals=0),
    )(pltpu.with_memory_space_constraint(weight, pltpu.HBM))


def terms_of(own, gate_weight, up_weight, down_weight):
    n, d = own.shape
    h = d // 2
    below, above = lax.optimization_barrier((shift(own, 0, 1), shift(own, 0, -1)))
    own_l, own_r = shift(own, 1, 0), shift(own, -1, 0)
    far = shift(below, 0, 1)
    near, own_l, own_r, gate_v, up_v, up_weight = lax.optimization_barrier(
        (jnp.concatenate([below, above], 0), own_l, own_r, fetched(gate_weight), fetched(up_weight, 0, 2), up_weight)
    )
    near_l, near_r = shift(near, 1, 0), shift(near, -1, 0)
    far, up_v2 = lax.optimization_barrier((far, fetched(up_weight, 1, 2)))
    weights = gate_v, up_v, up_v2
    (early,) = hidden_units((own, own_l, own_r, below, above, far), weights)
    far_l, far_r = lax.optimization_barrier((shift(far, 1, 0), shift(far, -1, 0)))
    near_l, near_r, early = lax.optimization_barrier((near_l, near_r, early))
    two_up = shift(jnp.concatenate([near_l[:n], own_l[:, :h]], 1), 1, 0)
    two_down = shift(jnp.concatenate([near_r[n:], own_r[:, h:]], 1), -1, 0)
    far_2up, far_2down = shift(far_l[:, :h], 1, 0), shift(far_r[:, h:], -1, 0)
    late, down_v = hidden_units((near_l, near_r, far_l, far_r), weights, down_weight)
    two_up, two_down = two_hops(two_up, two_down, far_2up, far_2down, weights, down_v)
    return *other_terms(early, late, down_v), two_up, two_down


def returned(own_here, own_left, own_right, near_here, far_here, near_left, near_right, far_left, far_right, two_up, two_down):
    n, d = own_here.shape
    h = d // 2
    two_up, two_down = lax.optimization_barrier((shift(two_up, 1, 0), shift(two_down, -1, 0)))
    far_up, far_down = two_up[:, d + h :], two_down[:, d + h :]
    far_right = jnp.concatenate([b16(far_right[:, :h] + f32(far_up)), b16(far_right[:, h:])], 1)
    far_left = jnp.concatenate([b16(far_left[:, :h]), b16(far_left[:, h:] + f32(far_down))], 1)
    far_p, far_m = shift(far_right, 1, 0), shift(far_left, -1, 0)
    near_right = jnp.concatenate([b16(near_right[:n] + f32(two_up[:, :d])), b16(near_right[n:])], 0)
    near_left = jnp.concatenate([b16(near_left[:n]), b16(near_left[n:] + f32(two_down[:, :d]))], 0)
    near_p, near_m = shift(near_right, 1, 0), shift(near_left, -1, 0)
    own_right = jnp.concatenate([b16(own_right[:, :h] + f32(two_up[:, d : d + h])), b16(own_right[:, h:])], 1)
    own_left = jnp.concatenate([b16(own_left[:, :h]), b16(own_left[:, h:] + f32(two_down[:, d : d + h]))], 1)
    own_right, own_left, near_p, near_m = lax.optimization_barrier((own_right, own_left, near_p, near_m))
    far_sum = shift(b16(far_here + f32(far_p) + f32(far_m)), 0, -1)
    own_p, own_m = shift(own_right, 1, 0), shift(own_left, -1, 0)
    near_sum = near_here + f32(near_p) + f32(near_m)
    from_below = shift(b16(near_sum[n:]), 0, 1)
    from_above = shift(b16(near_sum[:n] + f32(far_sum)), 0, -1)
    return own_here + f32(own_p) + f32(own_m) + f32(from_below) + f32(from_above)


def on_device(tokens, norm_gain, gate_weight, up_weight, down_weight):
    own = rms_normed(tokens, norm_gain)
    return b16(f32(tokens) + returned(*terms_of(own, gate_weight, up_weight, down_weight)))


def solution(mesh):
    return jax.shard_map(
        on_device,
        mesh=mesh,
        in_specs=(
            P(("dp", "tensor"), None),
            P(),
            P(None, "tensor"),
            P(None, "tensor"),
            P("tensor", None),
        ),
        out_specs=P(("dp", "tensor"), None),
        check_vma=False,
    )
```

```python
import jax
import jax.numpy as jnp
from jax import lax
from jax.experimental import pallas as pl
from jax.experimental.pallas import tpu as pltpu
from jax.sharding import PartitionSpec as P

SIDE = 4


def shift(block, dx, dz):
    pairs = []
    for part in range(lax.axis_size("dp")):
        way = 1 - 2 * (part % 2)
        for x in range(SIDE):
            for z in range(SIDE):
                there = (x + dx) % SIDE * SIDE + (z + way * dz) % SIDE
                pairs.append((part * SIDE**2 + x * SIDE + z, part * SIDE**2 + there))
    return lax.ppermute(block, ("dp", "tensor"), pairs)


def b16(v):
    return v.astype(jnp.bfloat16)


def f32(v):
    return v.astype(jnp.float32)


def rms_normed(rows, gain):
    def kernel(rows_ref, gain_ref, out_ref):
        held = f32(rows_ref[...])
        scale = lax.rsqrt(jnp.mean(held * held, axis=1, keepdims=True) + 1e-05)
        out_ref[...] = b16(held * scale * gain_ref[...])

    vmem = pl.BlockSpec(memory_space=pltpu.VMEM)
    return pl.pallas_call(
        kernel,
        out_shape=pltpu.VMEM(rows.shape, jnp.bfloat16),
        in_specs=[vmem] * 2,
        out_specs=vmem,
        compiler_params=pltpu.CompilerParams(vmem_limit_bytes=4 * 1024 * 1024),
    )(*[pltpu.with_memory_space_constraint(v, pltpu.HBM) for v in (rows, gain.reshape(1, -1))])


def placed(blocks):
    return [pltpu.with_memory_space_constraint(v, pltpu.VMEM) for v in blocks]


def hidden_of(rows, *weights):
    size, wide = weights[0].shape
    both = jnp.dot(rows[:, :size], weights[0][...], preferred_element_type=jnp.float32)
    for i, weight in enumerate(weights[1:], 1):
        both = both + jnp.dot(rows[:, i * size : (i + 1) * size], weight[...], preferred_element_type=jnp.float32)
    gate, up = both[:, : wide // 2], both[:, wide // 2 :]
    return b16(gate / (1.0 + jnp.exp(-gate)) * up)


def hidden_units(blocks, weights, down_weight=None):
    (n, d), ff = blocks[0].shape, weights[0].shape[1] // 2
    tall, held = sum(v.shape[0] for v in blocks), len(blocks)
    also = () if down_weight is None else (pltpu.with_memory_space_constraint(down_weight, pltpu.HBM),)

    def kernel(*refs):
        ins, ws, rest = refs[:held], refs[held : held + len(weights)], refs[held + len(weights) :]
        if also:
            source, out, target, rows, done = rest
            copy = pltpu.make_async_copy(source, target, done)
            copy.start()
        else:
            out, rows = rest
        at = 0
        for ref in ins:
            rows[at : at + ref.shape[0], :] = ref[...]
            at += ref.shape[0]
        out[...] = hidden_of(rows, *ws)
        if also:
            copy.wait()

    vmem, b = pl.BlockSpec(memory_space=pltpu.VMEM), jnp.bfloat16
    return pl.pallas_call(
        kernel,
        out_shape=[pltpu.VMEM((tall, ff), b)] + [pltpu.VMEM((ff, d), b) for _ in also],
        in_specs=[vmem] * (held + len(weights)) + [pl.BlockSpec(memory_space=pltpu.HBM) for _ in also],
        out_specs=[vmem] * (1 + len(also)),
        scratch_shapes=[pltpu.VMEM((tall, d), b)] + [pltpu.SemaphoreType.DMA for _ in also],
        compiler_params=pltpu.CompilerParams(vmem_limit_bytes=4 * 1024 * 1024),
        cost_estimate=pl.CostEstimate(flops=4 * tall * d * ff, bytes_accessed=2 * d * ff * len(also), transcendentals=tall * ff),
    )(*placed((*blocks, *weights)), *also)


def two_hops(two_up, two_down, far_up, far_down, weights, down_w):
    (n, h), (ff, d), step = far_up.shape, down_w.shape, 1024

    def kernel(two_up, two_down, far_up, far_down, w_0, w_1, w_2, down_w, out_up, out_down, rows, hidden):
        rows[:n, :] = two_up[:, :d]
        rows[n : 2 * n, :] = two_down[:, :d]
        rows[2 * n : 3 * n, :h] = two_up[:, d:]
        rows[2 * n : 3 * n, h:] = two_down[:, d:]
        rows[3 * n :, :h] = far_up[...]
        rows[3 * n :, h:] = far_down[...]
        hidden[...] = hidden_of(rows, w_0, w_1, w_2)
        for second in (False, True):
            target = out_down if second else out_up

            @pl.loop(0, h // step)
            def _(i):
                start = pl.multiple_of(i * step, step)
                cut = pl.ds(start + second * h, step)
                terms = b16(jnp.dot(hidden[...], down_w[:, cut], preferred_element_type=jnp.float32))
                out_up[:, cut] = terms[:n]
                out_down[:, cut] = terms[n : 2 * n]
                target[:, pl.ds(start + d, step)] = terms[2 * n : 3 * n]
                target[:, pl.ds(start + d + h, step)] = terms[3 * n :]

    vmem, b = pl.BlockSpec(memory_space=pltpu.VMEM), jnp.bfloat16
    return pl.pallas_call(
        kernel,
        out_shape=[pltpu.VMEM((n, 2 * d), b)] * 2,
        in_specs=[vmem] * 8,
        out_specs=[vmem] * 2,
        scratch_shapes=[pltpu.VMEM((4 * n, d), b), pltpu.VMEM((4 * n, ff), b)],
        compiler_params=pltpu.CompilerParams(vmem_limit_bytes=4 * 1024 * 1024),
        cost_estimate=pl.CostEstimate(flops=6 * 4 * n * d * ff, bytes_accessed=0, transcendentals=4 * n * ff),
    )(*placed((two_up, two_down, far_up, far_down, *weights, down_w)))


def other_terms(early, late, down_weight):
    n, (ff, d), step = early.shape[0] // 6, down_weight.shape, 1024
    tall = (1, 1, 1, 2, 1, 2, 2, 1, 1)

    def kernel(early, late, down_w, *rest):
        outs, held = rest[:-1], rest[-1]
        held[: 6 * n, :] = early[...]
        held[6 * n :, :] = late[...]

        @pl.loop(0, d // step)
        def _(i):
            cut = pl.ds(pl.multiple_of(i * step, step), step)
            terms = jnp.dot(held[...], down_w[:, cut], preferred_element_type=jnp.float32)
            at = 0
            for out, k in zip(outs, tall, strict=True):
                out[:, cut] = terms[at * n : (at + k) * n]
                at += k

    vmem = pl.BlockSpec(memory_space=pltpu.VMEM)
    return pl.pallas_call(
        kernel,
        out_shape=[pltpu.VMEM((k * n, d), jnp.float32) for k in tall],
        in_specs=[vmem] * 3,
        out_specs=[vmem] * 9,
        scratch_shapes=[pltpu.VMEM((12 * n, ff), jnp.bfloat16)],
        compiler_params=pltpu.CompilerParams(vmem_limit_bytes=4 * 1024 * 1024),
        cost_estimate=pl.CostEstimate(flops=2 * 12 * n * d * ff, bytes_accessed=0, transcendentals=0),
    )(*placed((early, late, down_weight)))


def fetched(gate_weight, up_weight, part, parts=3):
    (d, ff), size = gate_weight.shape, gate_weight.shape[0] // parts

    def kernel(gate, up, target, done):
        cut = pl.ds(part * size, size)
        copies = [
            pltpu.make_async_copy(gate.at[cut, :], target.at[:, pl.ds(0, ff)], done.at[0]),
            pltpu.make_async_copy(up.at[cut, :], target.at[:, pl.ds(ff, ff)], done.at[1]),
        ]
        for copy in copies:
            copy.start()
        for copy in copies:
            copy.wait()

    return pl.pallas_call(
        kernel,
        out_shape=pltpu.VMEM((size, 2 * ff), gate_weight.dtype),
        in_specs=[pl.BlockSpec(memory_space=pltpu.HBM)] * 2,
        out_specs=pl.BlockSpec(memory_space=pltpu.VMEM),
        scratch_shapes=[pltpu.SemaphoreType.DMA((2,))],
        compiler_params=pltpu.CompilerParams(vmem_limit_bytes=1024 * 1024),
        cost_estimate=pl.CostEstimate(flops=0, bytes_accessed=4 * size * ff, transcendentals=0),
    )(*[pltpu.with_memory_space_constraint(w, pltpu.HBM) for w in (gate_weight, up_weight)])


def terms_of(own, gate_weight, up_weight, down_weight):
    n, d = own.shape
    h = d // 2
    below, above = lax.optimization_barrier((shift(own, 0, 1), shift(own, 0, -1)))
    own_l, own_r = shift(own, 1, 0), shift(own, -1, 0)
    far = shift(below, 0, 1)
    pieces = [fetched(gate_weight, up_weight, i) for i in range(2)]
    near, own_l, own_r, gate_weight, *pieces = lax.optimization_barrier(
        (jnp.concatenate([below, above], 0), own_l, own_r, gate_weight, *pieces)
    )
    near_l, near_r = shift(near, 1, 0), shift(near, -1, 0)
    far, last = lax.optimization_barrier((far, fetched(gate_weight, up_weight, 2)))
    weights = *pieces, last
    (early,) = hidden_units((own, own_l, own_r, below, above, far), weights)
    far_l, far_r = lax.optimization_barrier((shift(far, 1, 0), shift(far, -1, 0)))
    near_l, near_r, early = lax.optimization_barrier((near_l, near_r, early))
    two_up = shift(jnp.concatenate([near_l[:n], own_l[:, :h]], 1), 1, 0)
    two_down = shift(jnp.concatenate([near_r[n:], own_r[:, h:]], 1), -1, 0)
    far_2up, far_2down = shift(far_l[:, :h], 1, 0), shift(far_r[:, h:], -1, 0)
    late, down_v = hidden_units((near_l, near_r, far_l, far_r), weights, down_weight)
    two_up, two_down = two_hops(two_up, two_down, far_2up, far_2down, weights, down_v)
    return *other_terms(early, late, down_v), two_up, two_down


def returned(own_here, own_left, own_right, near_here, far_here, near_left, near_right, far_left, far_right, two_up, two_down):
    n, d = own_here.shape
    h = d // 2
    two_up, two_down = lax.optimization_barrier((shift(two_up, 1, 0), shift(two_down, -1, 0)))
    far_up, far_down = two_up[:, d + h :], two_down[:, d + h :]
    far_right = jnp.concatenate([b16(far_right[:, :h] + f32(far_up)), b16(far_right[:, h:])], 1)
    far_left = jnp.concatenate([b16(far_left[:, :h]), b16(far_left[:, h:] + f32(far_down))], 1)
    far_p, far_m = shift(far_right, 1, 0), shift(far_left, -1, 0)
    near_right = jnp.concatenate([b16(near_right[:n] + f32(two_up[:, :d])), b16(near_right[n:])], 0)
    near_left = jnp.concatenate([b16(near_left[:n]), b16(near_left[n:] + f32(two_down[:, :d]))], 0)
    near_p, near_m = shift(near_right, 1, 0), shift(near_left, -1, 0)
    own_right = jnp.concatenate([b16(own_right[:, :h] + f32(two_up[:, d : d + h])), b16(own_right[:, h:])], 1)
    own_left = jnp.concatenate([b16(own_left[:, :h]), b16(own_left[:, h:] + f32(two_down[:, d : d + h]))], 1)
    own_right, own_left, near_p, near_m = lax.optimization_barrier((own_right, own_left, near_p, near_m))
    far_sum = shift(b16(far_here + f32(far_p) + f32(far_m)), 0, 2)
    own_p, own_m = shift(own_right, 1, 0), shift(own_left, -1, 0)
    near_sum = b16(near_here + f32(near_p) + f32(near_m))
    from_below, from_above = shift(near_sum[n:], 0, 1), shift(near_sum[:n], 0, -1)
    return own_here + f32(own_p) + f32(own_m) + f32(far_sum) + f32(from_below) + f32(from_above)


def on_device(tokens, norm_gain, gate_weight, up_weight, down_weight):
    own = rms_normed(tokens, norm_gain)
    return b16(f32(tokens) + returned(*terms_of(own, gate_weight, up_weight, down_weight)))


def solution(mesh):
    return jax.shard_map(
        on_device,
        mesh=mesh,
        in_specs=(
            P(("dp", "tensor"), None),
            P(),
            P(None, "tensor"),
            P(None, "tensor"),
            P("tensor", None),
        ),
        out_specs=P(("dp", "tensor"), None),
        check_vma=False,
    )
```

```python
import jax
import jax.numpy as jnp
from jax import lax
from jax.experimental import pallas as pl
from jax.experimental.pallas import tpu as pltpu
from jax.sharding import PartitionSpec as P

SIDE = 4


def shift(block, dx, dz):
    pairs = []
    for part in range(lax.axis_size("dp")):
        way = 1 - 2 * (part % 2)
        for x in range(SIDE):
            for z in range(SIDE):
                there = (x + dx) % SIDE * SIDE + (z + way * dz) % SIDE
                pairs.append((part * SIDE**2 + x * SIDE + z, part * SIDE**2 + there))
    return lax.ppermute(block, ("dp", "tensor"), pairs)


def b16(v):
    return v.astype(jnp.bfloat16)


def f32(v):
    return v.astype(jnp.float32)


def rms_normed(rows, gain):
    def kernel(rows_ref, gain_ref, out_ref):
        held = f32(rows_ref[...])
        scale = lax.rsqrt(jnp.mean(held * held, axis=1, keepdims=True) + 1e-05)
        out_ref[...] = b16(held * scale * gain_ref[...])

    vmem = pl.BlockSpec(memory_space=pltpu.VMEM)
    return pl.pallas_call(
        kernel,
        out_shape=pltpu.VMEM(rows.shape, jnp.bfloat16),
        in_specs=[vmem] * 2,
        out_specs=vmem,
        compiler_params=pltpu.CompilerParams(vmem_limit_bytes=4 * 1024 * 1024),
    )(*[pltpu.with_memory_space_constraint(v, pltpu.HBM) for v in (rows, gain.reshape(1, -1))])


def placed(blocks):
    return [pltpu.with_memory_space_constraint(v, pltpu.VMEM) for v in blocks]


def hidden_of(rows, gate_w, up_w, up_w2):
    half = up_w.shape[0]
    gate = jnp.dot(rows[...], gate_w[...], preferred_element_type=jnp.float32)
    up = jnp.dot(rows[:, :half], up_w[...], preferred_element_type=jnp.float32)
    up = up + jnp.dot(rows[:, half:], up_w2[...], preferred_element_type=jnp.float32)
    return b16(gate / (1.0 + jnp.exp(-gate)) * up)


def hidden_units(blocks, weights, down_weight=None):
    (n, d), ff = blocks[0].shape, weights[0].shape[1]
    tall, held = sum(v.shape[0] for v in blocks), len(blocks)
    also = () if down_weight is None else (pltpu.with_memory_space_constraint(down_weight, pltpu.HBM),)

    def kernel(*refs):
        ins, ws, rest = refs[:held], refs[held : held + len(weights)], refs[held + len(weights) :]
        if also:
            source, out, target, rows, done = rest
            copy = pltpu.make_async_copy(source, target, done)
            copy.start()
        else:
            out, rows = rest
        at = 0
        for ref in ins:
            rows[at : at + ref.shape[0], :] = ref[...]
            at += ref.shape[0]
        out[...] = hidden_of(rows, *ws)
        if also:
            copy.wait()

    vmem, b = pl.BlockSpec(memory_space=pltpu.VMEM), jnp.bfloat16
    return pl.pallas_call(
        kernel,
        out_shape=[pltpu.VMEM((tall, ff), b)] + [pltpu.VMEM((ff, d), b) for _ in also],
        in_specs=[vmem] * (held + len(weights)) + [pl.BlockSpec(memory_space=pltpu.HBM) for _ in also],
        out_specs=[vmem] * (1 + len(also)),
        scratch_shapes=[pltpu.VMEM((tall, d), b)] + [pltpu.SemaphoreType.DMA for _ in also],
        compiler_params=pltpu.CompilerParams(vmem_limit_bytes=8 * 1024 * 1024),
        cost_estimate=pl.CostEstimate(flops=4 * tall * d * ff, bytes_accessed=2 * d * ff * len(also), transcendentals=tall * ff),
    )(*placed((*blocks, *weights)), *also)


def two_hops(two_up, two_down, far_up, far_down, weights, down_w):
    (n, h), (ff, d), step = far_up.shape, down_w.shape, 1024

    def kernel(two_up, two_down, far_up, far_down, gate_w, up_w, up_w2, down_w, out_up, out_down, rows, hidden):
        rows[:n, :] = two_up[:, :d]
        rows[n : 2 * n, :] = two_down[:, :d]
        rows[2 * n : 3 * n, :h] = two_up[:, d:]
        rows[2 * n : 3 * n, h:] = two_down[:, d:]
        rows[3 * n :, :h] = far_up[...]
        rows[3 * n :, h:] = far_down[...]
        hidden[...] = hidden_of(rows, gate_w, up_w, up_w2)
        for second in (False, True):
            target = out_down if second else out_up

            @pl.loop(0, h // step)
            def _(i):
                start = pl.multiple_of(i * step, step)
                cut = pl.ds(start + second * h, step)
                terms = b16(jnp.dot(hidden[...], down_w[:, cut], preferred_element_type=jnp.float32))
                out_up[:, cut] = terms[:n]
                out_down[:, cut] = terms[n : 2 * n]
                target[:, pl.ds(start + d, step)] = terms[2 * n : 3 * n]
                target[:, pl.ds(start + d + h, step)] = terms[3 * n :]

    vmem, b = pl.BlockSpec(memory_space=pltpu.VMEM), jnp.bfloat16
    return pl.pallas_call(
        kernel,
        out_shape=[pltpu.VMEM((n, 2 * d), b)] * 2,
        in_specs=[vmem] * 8,
        out_specs=[vmem] * 2,
        scratch_shapes=[pltpu.VMEM((4 * n, d), b), pltpu.VMEM((4 * n, ff), b)],
        compiler_params=pltpu.CompilerParams(vmem_limit_bytes=8 * 1024 * 1024),
        cost_estimate=pl.CostEstimate(flops=6 * 4 * n * d * ff, bytes_accessed=0, transcendentals=4 * n * ff),
    )(*placed((two_up, two_down, far_up, far_down, *weights, down_w)))


def other_terms(early, late, down_weight):
    n, (ff, d), step = early.shape[0] // 6, down_weight.shape, 1024
    tall = (1, 1, 1, 2, 1, 2, 2, 1, 1)

    def kernel(early, late, down_w, *rest):
        outs, held = rest[:-1], rest[-1]
        held[: 6 * n, :] = early[...]
        held[6 * n :, :] = late[...]

        @pl.loop(0, d // step)
        def _(i):
            cut = pl.ds(pl.multiple_of(i * step, step), step)
            terms = jnp.dot(held[...], down_w[:, cut], preferred_element_type=jnp.float32)
            at = 0
            for out, k in zip(outs, tall, strict=True):
                out[:, cut] = terms[at * n : (at + k) * n]
                at += k

    vmem = pl.BlockSpec(memory_space=pltpu.VMEM)
    return pl.pallas_call(
        kernel,
        out_shape=[pltpu.VMEM((k * n, d), jnp.float32) for k in tall],
        in_specs=[vmem] * 3,
        out_specs=[vmem] * 9,
        scratch_shapes=[pltpu.VMEM((12 * n, ff), jnp.bfloat16)],
        compiler_params=pltpu.CompilerParams(vmem_limit_bytes=8 * 1024 * 1024),
        cost_estimate=pl.CostEstimate(flops=2 * 12 * n * d * ff, bytes_accessed=0, transcendentals=0),
    )(*placed((early, late, down_weight)))


def fetched(weight, part=0, parts=1):
    size = weight.shape[0] // parts

    def kernel(source, target, done):
        copy = pltpu.make_async_copy(source.at[pl.ds(part * size, size), :], target, done)
        copy.start()
        copy.wait()

    return pl.pallas_call(
        kernel,
        out_shape=pltpu.VMEM((size, weight.shape[1]), weight.dtype),
        in_specs=[pl.BlockSpec(memory_space=pltpu.HBM)],
        out_specs=pl.BlockSpec(memory_space=pltpu.VMEM),
        scratch_shapes=[pltpu.SemaphoreType.DMA],
        compiler_params=pltpu.CompilerParams(vmem_limit_bytes=1024 * 1024),
        cost_estimate=pl.CostEstimate(flops=0, bytes_accessed=2 * size * weight.shape[1], transcendentals=0),
    )(pltpu.with_memory_space_constraint(weight, pltpu.HBM))


def terms_of(own, gate_weight, up_weight, down_weight):
    n, d = own.shape
    h = d // 2
    below, above = lax.optimization_barrier((shift(own, 0, 1), shift(own, 0, -1)))
    own_l, own_r = shift(own, 1, 0), shift(own, -1, 0)
    far = shift(below, 0, 1)
    near, own_l, own_r, gate_v, up_v, up_weight = lax.optimization_barrier(
        (jnp.concatenate([below, above], 0), own_l, own_r, fetched(gate_weight), fetched(up_weight, 0, 2), up_weight)
    )
    near_l, near_r = shift(near, 1, 0), shift(near, -1, 0)
    far, up_v2 = lax.optimization_barrier((far, fetched(up_weight, 1, 2)))
    weights = gate_v, up_v, up_v2
    (early,) = hidden_units((own, own_l, own_r, below, above, far), weights)
    far_l, far_r = lax.optimization_barrier((shift(far, 1, 0), shift(far, -1, 0)))
    near_l, near_r, early = lax.optimization_barrier((near_l, near_r, early))
    two_up = shift(jnp.concatenate([near_l[:n], own_l[:, :h]], 1), 1, 0)
    two_down = shift(jnp.concatenate([near_r[n:], own_r[:, h:]], 1), -1, 0)
    far_2up, far_2down = shift(far_l[:, :h], 1, 0), shift(far_r[:, h:], -1, 0)
    late, down_v = hidden_units((near_l, near_r, far_l, far_r), weights, down_weight)
    two_up, two_down = two_hops(two_up, two_down, far_2up, far_2down, weights, down_v)
    return *other_terms(early, late, down_v), two_up, two_down


def returned(own_here, own_left, own_right, near_here, far_here, near_left, near_right, far_left, far_right, two_up, two_down):
    n, d = own_here.shape
    h = d // 2
    two_up, two_down = lax.optimization_barrier((shift(two_up, 1, 0), shift(two_down, -1, 0)))
    far_up, far_down = two_up[:, d + h :], two_down[:, d + h :]
    far_right = jnp.concatenate([b16(far_right[:, :h] + f32(far_up)), b16(far_right[:, h:])], 1)
    far_left = jnp.concatenate([b16(far_left[:, :h]), b16(far_left[:, h:] + f32(far_down))], 1)
    far_p, far_m = shift(far_right, 1, 0), shift(far_left, -1, 0)
    near_right = jnp.concatenate([b16(near_right[:n] + f32(two_up[:, :d])), b16(near_right[n:])], 0)
    near_left = jnp.concatenate([b16(near_left[:n]), b16(near_left[n:] + f32(two_down[:, :d]))], 0)
    near_p, near_m = shift(near_right, 1, 0), shift(near_left, -1, 0)
    own_right = jnp.concatenate([b16(own_right[:, :h] + f32(two_up[:, d : d + h])), b16(own_right[:, h:])], 1)
    own_left = jnp.concatenate([b16(own_left[:, :h]), b16(own_left[:, h:] + f32(two_down[:, d : d + h]))], 1)
    near_p, near_m = lax.optimization_barrier((near_p, near_m))
    far_p, far_m, _, _ = lax.optimization_barrier((far_p, far_m, near_p, near_m))
    far_sum = shift(b16(far_here + f32(far_p) + f32(far_m)), 0, 2)
    own_right, own_left, far_p, far_m = lax.optimization_barrier((own_right, own_left, far_p, far_m))
    own_p, own_m = shift(own_right, 1, 0), shift(own_left, -1, 0)
    near_sum = b16(near_here + f32(near_p) + f32(near_m))
    from_below, from_above = shift(near_sum[n:], 0, 1), shift(near_sum[:n], 0, -1)
    return own_here + f32(from_below) + f32(from_above) + f32(far_sum) + f32(own_p) + f32(own_m)


def on_device(tokens, norm_gain, gate_weight, up_weight, down_weight):
    own = rms_normed(tokens, norm_gain)
    return b16(f32(tokens) + returned(*terms_of(own, gate_weight, up_weight, down_weight)))


def solution(mesh):
    return jax.shard_map(
        on_device,
        mesh=mesh,
        in_specs=(
            P(("dp", "tensor"), None),
            P(),
            P(None, "tensor"),
            P(None, "tensor"),
            P("tensor", None),
        ),
        out_specs=P(("dp", "tensor"), None),
        check_vma=False,
    )
```

```python
import jax
import jax.numpy as jnp
from jax import lax
from jax.experimental import pallas as pl
from jax.experimental.pallas import tpu as pltpu
from jax.sharding import PartitionSpec as P

SIDE = 4


def shift(block, dx, dz):
    pairs = []
    for part in range(lax.axis_size("dp")):
        way = 1 - 2 * (part % 2)
        for x in range(SIDE):
            for z in range(SIDE):
                there = (x + dx) % SIDE * SIDE + (z + way * dz) % SIDE
                pairs.append((part * SIDE**2 + x * SIDE + z, part * SIDE**2 + there))
    return lax.ppermute(block, ("dp", "tensor"), pairs)


def b16(v):
    return v.astype(jnp.bfloat16)


def f32(v):
    return v.astype(jnp.float32)


def rms_normed(rows, gain):
    def kernel(rows_ref, gain_ref, out_ref):
        held = f32(rows_ref[...])
        scale = lax.rsqrt(jnp.mean(held * held, axis=1, keepdims=True) + 1e-05)
        out_ref[...] = b16(held * scale * gain_ref[...])

    vmem = pl.BlockSpec(memory_space=pltpu.VMEM)
    return pl.pallas_call(
        kernel,
        out_shape=pltpu.VMEM(rows.shape, jnp.bfloat16),
        in_specs=[vmem] * 2,
        out_specs=vmem,
        compiler_params=pltpu.CompilerParams(vmem_limit_bytes=4 * 1024 * 1024),
    )(*[pltpu.with_memory_space_constraint(v, pltpu.HBM) for v in (rows, gain.reshape(1, -1))])


def placed(blocks):
    return [pltpu.with_memory_space_constraint(v, pltpu.VMEM) for v in blocks]


def hidden_of(rows, gate_w, up_w, up_w2):
    half = up_w.shape[0]
    gate = jnp.dot(rows[...], gate_w[...], preferred_element_type=jnp.float32)
    up = jnp.dot(rows[:, :half], up_w[...], preferred_element_type=jnp.float32)
    up = up + jnp.dot(rows[:, half:], up_w2[...], preferred_element_type=jnp.float32)
    return b16(gate / (1.0 + jnp.exp(-gate)) * up)


def hidden_units(blocks, weights, down_weight=None):
    (n, d), ff = blocks[0].shape, weights[0].shape[1]
    tall, held = sum(v.shape[0] for v in blocks), len(blocks)
    also = () if down_weight is None else (pltpu.with_memory_space_constraint(down_weight, pltpu.HBM),)

    def kernel(*refs):
        ins, ws, rest = refs[:held], refs[held : held + len(weights)], refs[held + len(weights) :]
        if also:
            source, out, target, rows, done = rest
            copy = pltpu.make_async_copy(source, target, done)
            copy.start()
        else:
            out, rows = rest
        at = 0
        for ref in ins:
            rows[at : at + ref.shape[0], :] = ref[...]
            at += ref.shape[0]
        out[...] = hidden_of(rows, *ws)
        if also:
            copy.wait()

    vmem, b = pl.BlockSpec(memory_space=pltpu.VMEM), jnp.bfloat16
    return pl.pallas_call(
        kernel,
        out_shape=[pltpu.VMEM((tall, ff), b)] + [pltpu.VMEM((ff, d), b) for _ in also],
        in_specs=[vmem] * (held + len(weights)) + [pl.BlockSpec(memory_space=pltpu.HBM) for _ in also],
        out_specs=[vmem] * (1 + len(also)),
        scratch_shapes=[pltpu.VMEM((tall, d), b)] + [pltpu.SemaphoreType.DMA for _ in also],
        compiler_params=pltpu.CompilerParams(vmem_limit_bytes=8 * 1024 * 1024),
        cost_estimate=pl.CostEstimate(flops=4 * tall * d * ff, bytes_accessed=2 * d * ff * len(also), transcendentals=tall * ff),
    )(*placed((*blocks, *weights)), *also)


def two_hops(two_up, two_down, far_up, far_down, weights, down_w):
    (n, h), (ff, d) = far_up.shape, down_w.shape

    def kernel(two_up, two_down, far_up, far_down, gate_w, up_w, up_w2, down_w, out_up, out_down, rows, hidden):
        rows[:n, :] = two_up[:, :d]
        rows[n : 2 * n, :] = two_down[:, :d]
        rows[2 * n : 3 * n, :h] = two_up[:, d:]
        rows[2 * n : 3 * n, h:] = two_down[:, d:]
        rows[3 * n :, :h] = far_up[...]
        rows[3 * n :, h:] = far_down[...]
        hidden[...] = hidden_of(rows, gate_w, up_w, up_w2)
        for second in (False, True):
            target = out_down if second else out_up

            cut = pl.ds(second * h, h)
            terms = b16(jnp.dot(hidden[...], down_w[:, cut], preferred_element_type=jnp.float32))
            out_up[:, cut] = terms[:n]
            out_down[:, cut] = terms[n : 2 * n]
            target[:, pl.ds(d, h)] = terms[2 * n : 3 * n]
            target[:, pl.ds(d + h, h)] = terms[3 * n :]

    vmem, b = pl.BlockSpec(memory_space=pltpu.VMEM), jnp.bfloat16
    return pl.pallas_call(
        kernel,
        out_shape=[pltpu.VMEM((n, 2 * d), b)] * 2,
        in_specs=[vmem] * 8,
        out_specs=[vmem] * 2,
        scratch_shapes=[pltpu.VMEM((4 * n, d), b), pltpu.VMEM((4 * n, ff), b)],
        compiler_params=pltpu.CompilerParams(vmem_limit_bytes=8 * 1024 * 1024),
        cost_estimate=pl.CostEstimate(flops=6 * 4 * n * d * ff, bytes_accessed=0, transcendentals=4 * n * ff),
    )(*placed((two_up, two_down, far_up, far_down, *weights, down_w)))


def other_terms(early, late, down_weight):
    n, (ff, d), step = early.shape[0] // 6, down_weight.shape, 1024
    tall = (1, 1, 1, 2, 1, 2, 2, 1, 1)

    def kernel(early, late, down_w, *rest):
        outs, held = rest[:-1], rest[-1]
        held[: 6 * n, :] = early[...]
        held[6 * n :, :] = late[...]

        @pl.loop(0, d // step)
        def _(i):
            cut = pl.ds(pl.multiple_of(i * step, step), step)
            terms = jnp.dot(held[...], down_w[:, cut], preferred_element_type=jnp.float32)
            at = 0
            for out, k in zip(outs, tall, strict=True):
                out[:, cut] = terms[at * n : (at + k) * n]
                at += k

    vmem = pl.BlockSpec(memory_space=pltpu.VMEM)
    return pl.pallas_call(
        kernel,
        out_shape=[pltpu.VMEM((k * n, d), jnp.float32) for k in tall],
        in_specs=[vmem] * 3,
        out_specs=[vmem] * 9,
        scratch_shapes=[pltpu.VMEM((12 * n, ff), jnp.bfloat16)],
        compiler_params=pltpu.CompilerParams(vmem_limit_bytes=8 * 1024 * 1024),
        cost_estimate=pl.CostEstimate(flops=2 * 12 * n * d * ff, bytes_accessed=0, transcendentals=0),
    )(*placed((early, late, down_weight)))


def fetched(weight, part=0, parts=1):
    size = weight.shape[0] // parts

    def kernel(source, target, done):
        copy = pltpu.make_async_copy(source.at[pl.ds(part * size, size), :], target, done)
        copy.start()
        copy.wait()

    return pl.pallas_call(
        kernel,
        out_shape=pltpu.VMEM((size, weight.shape[1]), weight.dtype),
        in_specs=[pl.BlockSpec(memory_space=pltpu.HBM)],
        out_specs=pl.BlockSpec(memory_space=pltpu.VMEM),
        scratch_shapes=[pltpu.SemaphoreType.DMA],
        compiler_params=pltpu.CompilerParams(vmem_limit_bytes=1024 * 1024),
        cost_estimate=pl.CostEstimate(flops=0, bytes_accessed=2 * size * weight.shape[1], transcendentals=0),
    )(pltpu.with_memory_space_constraint(weight, pltpu.HBM))


def terms_of(own, gate_weight, up_weight, down_weight):
    n, d = own.shape
    h = d // 2
    below, above = lax.optimization_barrier((shift(own, 0, 1), shift(own, 0, -1)))
    own_l, own_r = shift(own, 1, 0), shift(own, -1, 0)
    far = shift(below, 0, 1)
    near, own_l, own_r, gate_v, up_v, up_weight = lax.optimization_barrier(
        (jnp.concatenate([below, above], 0), own_l, own_r, fetched(gate_weight), fetched(up_weight, 0, 2), up_weight)
    )
    near_l, near_r = shift(near, 1, 0), shift(near, -1, 0)
    far, up_v2 = lax.optimization_barrier((far, fetched(up_weight, 1, 2)))
    weights = gate_v, up_v, up_v2
    (early,) = hidden_units((own, own_l, own_r, below, above, far), weights)
    far_l, far_r = lax.optimization_barrier((shift(far, 1, 0), shift(far, -1, 0)))
    near_l, near_r, early = lax.optimization_barrier((near_l, near_r, early))
    two_up = shift(jnp.concatenate([near_l[:n], own_l[:, :h]], 1), 1, 0)
    two_down = shift(jnp.concatenate([near_r[n:], own_r[:, h:]], 1), -1, 0)
    far_2up, far_2down = shift(far_l[:, :h], 1, 0), shift(far_r[:, h:], -1, 0)
    late, down_v = hidden_units((near_l, near_r, far_l, far_r), weights, down_weight)
    two_up, two_down = two_hops(two_up, two_down, far_2up, far_2down, weights, down_v)
    return *other_terms(early, late, down_v), two_up, two_down


def returned(own_here, own_left, own_right, near_here, far_here, near_left, near_right, far_left, far_right, two_up, two_down):
    n, d = own_here.shape
    h = d // 2
    two_up, two_down = lax.optimization_barrier((shift(two_up, 1, 0), shift(two_down, -1, 0)))
    far_up, far_down = two_up[:, d + h :], two_down[:, d + h :]
    far_right = jnp.concatenate([b16(far_right[:, :h] + f32(far_up)), b16(far_right[:, h:])], 1)
    far_left = jnp.concatenate([b16(far_left[:, :h]), b16(far_left[:, h:] + f32(far_down))], 1)
    far_p, far_m = shift(far_right, 1, 0), shift(far_left, -1, 0)
    near_right = jnp.concatenate([b16(near_right[:n] + f32(two_up[:, :d])), b16(near_right[n:])], 0)
    near_left = jnp.concatenate([b16(near_left[:n]), b16(near_left[n:] + f32(two_down[:, :d]))], 0)
    near_p, near_m = shift(near_right, 1, 0), shift(near_left, -1, 0)
    own_right = jnp.concatenate([b16(own_right[:, :h] + f32(two_up[:, d : d + h])), b16(own_right[:, h:])], 1)
    own_left = jnp.concatenate([b16(own_left[:, :h]), b16(own_left[:, h:] + f32(two_down[:, d : d + h]))], 1)
    own_right, own_left, near_p, near_m = lax.optimization_barrier((own_right, own_left, near_p, near_m))
    far_sum = shift(b16(far_here + f32(far_p) + f32(far_m)), 0, 2)
    own_p, own_m = shift(own_right, 1, 0), shift(own_left, -1, 0)
    near_sum = b16(near_here + f32(near_p) + f32(near_m))
    from_below, from_above = shift(near_sum[n:], 0, 1), shift(near_sum[:n], 0, -1)
    return own_here + f32(own_p) + f32(own_m) + f32(far_sum) + f32(from_below) + f32(from_above)


def on_device(tokens, norm_gain, gate_weight, up_weight, down_weight):
    own = rms_normed(tokens, norm_gain)
    return b16(f32(tokens) + returned(*terms_of(own, gate_weight, up_weight, down_weight)))


def solution(mesh):
    return jax.shard_map(
        on_device,
        mesh=mesh,
        in_specs=(
            P(("dp", "tensor"), None),
            P(),
            P(None, "tensor"),
            P(None, "tensor"),
            P("tensor", None),
        ),
        out_specs=P(("dp", "tensor"), None),
        check_vma=False,
    )
```

```python
import jax
import jax.numpy as jnp
from jax import lax
from jax.experimental import pallas as pl
from jax.experimental.pallas import tpu as pltpu
from jax.sharding import PartitionSpec as P

SIDE = 4


def shift(block, dx, dz):
    pairs = []
    for part in range(lax.axis_size("dp")):
        way = 1 - 2 * (part % 2)
        for x in range(SIDE):
            for z in range(SIDE):
                there = (x + dx) % SIDE * SIDE + (z + way * dz) % SIDE
                pairs.append((part * SIDE**2 + x * SIDE + z, part * SIDE**2 + there))
    return lax.ppermute(block, ("dp", "tensor"), pairs)


def b16(v):
    return v.astype(jnp.bfloat16)


def f32(v):
    return v.astype(jnp.float32)


def rms_normed(rows, gain):
    def kernel(rows_ref, gain_ref, out_ref):
        held = f32(rows_ref[...])
        scale = lax.rsqrt(jnp.mean(held * held, axis=1, keepdims=True) + 1e-05)
        out_ref[...] = b16(held * scale * gain_ref[...])

    vmem = pl.BlockSpec(memory_space=pltpu.VMEM)
    return pl.pallas_call(
        kernel,
        out_shape=pltpu.VMEM(rows.shape, jnp.bfloat16),
        in_specs=[vmem] * 2,
        out_specs=vmem,
        compiler_params=pltpu.CompilerParams(vmem_limit_bytes=4 * 1024 * 1024),
    )(*[pltpu.with_memory_space_constraint(v, pltpu.HBM) for v in (rows, gain.reshape(1, -1))])


def placed(blocks):
    return [pltpu.with_memory_space_constraint(v, pltpu.VMEM) for v in blocks]


def hidden_of(rows, gate_w, up_w, up_w2):
    half = up_w.shape[0]
    gate = jnp.dot(rows[...], gate_w[...], preferred_element_type=jnp.float32)
    up = jnp.dot(rows[:, :half], up_w[...], preferred_element_type=jnp.float32)
    up = up + jnp.dot(rows[:, half:], up_w2[...], preferred_element_type=jnp.float32)
    return b16(gate / (1.0 + jnp.exp(-gate)) * up)


def hidden_units(blocks, weights, down_weight=None):
    (n, d), ff = blocks[0].shape, weights[0].shape[1]
    tall, held = sum(v.shape[0] for v in blocks), len(blocks)
    also = () if down_weight is None else (pltpu.with_memory_space_constraint(down_weight, pltpu.HBM),)

    def kernel(*refs):
        ins, ws, rest = refs[:held], refs[held : held + len(weights)], refs[held + len(weights) :]
        if also:
            source, out, target, rows, done = rest
            copy = pltpu.make_async_copy(source, target, done)
            copy.start()
        else:
            out, rows = rest
        at = 0
        for ref in ins:
            rows[at : at + ref.shape[0], :] = ref[...]
            at += ref.shape[0]
        out[...] = hidden_of(rows, *ws)
        if also:
            copy.wait()

    vmem, b = pl.BlockSpec(memory_space=pltpu.VMEM), jnp.bfloat16
    return pl.pallas_call(
        kernel,
        out_shape=[pltpu.VMEM((tall, ff), b)] + [pltpu.VMEM((ff, d), b) for _ in also],
        in_specs=[vmem] * (held + len(weights)) + [pl.BlockSpec(memory_space=pltpu.HBM) for _ in also],
        out_specs=[vmem] * (1 + len(also)),
        scratch_shapes=[pltpu.VMEM((tall, d), b)] + [pltpu.SemaphoreType.DMA for _ in also],
        compiler_params=pltpu.CompilerParams(vmem_limit_bytes=8 * 1024 * 1024),
        cost_estimate=pl.CostEstimate(flops=4 * tall * d * ff, bytes_accessed=2 * d * ff * len(also), transcendentals=tall * ff),
    )(*placed((*blocks, *weights)), *also)


def two_hops(two_up, two_down, far_up, far_down, weights, down_w):
    (n, h), (ff, d) = far_up.shape, down_w.shape

    def kernel(two_up, two_down, far_up, far_down, gate_w, up_w, up_w2, down_w, out_up, out_down, rows, hidden):
        rows[:n, :] = two_up[:, :d]
        rows[n : 2 * n, :] = two_down[:, :d]
        rows[2 * n : 3 * n, :h] = two_up[:, d:]
        rows[2 * n : 3 * n, h:] = two_down[:, d:]
        rows[3 * n :, :h] = far_up[...]
        rows[3 * n :, h:] = far_down[...]
        hidden[...] = hidden_of(rows, gate_w, up_w, up_w2)
        terms = b16(jnp.dot(hidden[...], down_w[...], preferred_element_type=jnp.float32))
        out_up[:, :d] = terms[:n]
        out_down[:, :d] = terms[n : 2 * n]
        for side, target in ((0, out_up), (h, out_down)):
            target[:, d : d + h] = terms[2 * n : 3 * n, side : side + h]
            target[:, d + h :] = terms[3 * n :, side : side + h]

    vmem, b = pl.BlockSpec(memory_space=pltpu.VMEM), jnp.bfloat16
    return pl.pallas_call(
        kernel,
        out_shape=[pltpu.VMEM((n, 2 * d), b)] * 2,
        in_specs=[vmem] * 8,
        out_specs=[vmem] * 2,
        scratch_shapes=[pltpu.VMEM((4 * n, d), b), pltpu.VMEM((4 * n, ff), b)],
        compiler_params=pltpu.CompilerParams(vmem_limit_bytes=8 * 1024 * 1024),
        cost_estimate=pl.CostEstimate(flops=6 * 4 * n * d * ff, bytes_accessed=0, transcendentals=4 * n * ff),
    )(*placed((two_up, two_down, far_up, far_down, *weights, down_w)))


def other_terms(early, late, down_weight):
    n, (ff, d), step = early.shape[0] // 6, down_weight.shape, 1024
    tall = (1, 1, 1, 2, 1, 2, 2, 1, 1)

    def kernel(early, late, down_w, *rest):
        outs, held = rest[:-1], rest[-1]
        held[: 6 * n, :] = early[...]
        held[6 * n :, :] = late[...]

        @pl.loop(0, d // step)
        def _(i):
            cut = pl.ds(pl.multiple_of(i * step, step), step)
            terms = jnp.dot(held[...], down_w[:, cut], preferred_element_type=jnp.float32)
            at = 0
            for out, k in zip(outs, tall, strict=True):
                out[:, cut] = terms[at * n : (at + k) * n]
                at += k

    vmem = pl.BlockSpec(memory_space=pltpu.VMEM)
    return pl.pallas_call(
        kernel,
        out_shape=[pltpu.VMEM((k * n, d), jnp.float32) for k in tall],
        in_specs=[vmem] * 3,
        out_specs=[vmem] * 9,
        scratch_shapes=[pltpu.VMEM((12 * n, ff), jnp.bfloat16)],
        compiler_params=pltpu.CompilerParams(vmem_limit_bytes=8 * 1024 * 1024),
        cost_estimate=pl.CostEstimate(flops=2 * 12 * n * d * ff, bytes_accessed=0, transcendentals=0),
    )(*placed((early, late, down_weight)))


def fetched(weight, part=0, parts=1):
    size = weight.shape[0] // parts

    def kernel(source, target, done):
        copy = pltpu.make_async_copy(source.at[pl.ds(part * size, size), :], target, done)
        copy.start()
        copy.wait()

    return pl.pallas_call(
        kernel,
        out_shape=pltpu.VMEM((size, weight.shape[1]), weight.dtype),
        in_specs=[pl.BlockSpec(memory_space=pltpu.HBM)],
        out_specs=pl.BlockSpec(memory_space=pltpu.VMEM),
        scratch_shapes=[pltpu.SemaphoreType.DMA],
        compiler_params=pltpu.CompilerParams(vmem_limit_bytes=1024 * 1024),
        cost_estimate=pl.CostEstimate(flops=0, bytes_accessed=2 * size * weight.shape[1], transcendentals=0),
    )(pltpu.with_memory_space_constraint(weight, pltpu.HBM))


def terms_of(own, gate_weight, up_weight, down_weight):
    n, d = own.shape
    h = d // 2
    below, above = lax.optimization_barrier((shift(own, 0, 1), shift(own, 0, -1)))
    own_l, own_r = shift(own, 1, 0), shift(own, -1, 0)
    far = shift(below, 0, 1)
    near, own_l, own_r, gate_v, up_v, up_weight = lax.optimization_barrier(
        (jnp.concatenate([below, above], 0), own_l, own_r, fetched(gate_weight), fetched(up_weight, 0, 2), up_weight)
    )
    near_l, near_r = shift(near, 1, 0), shift(near, -1, 0)
    far, up_v2 = lax.optimization_barrier((far, fetched(up_weight, 1, 2)))
    weights = gate_v, up_v, up_v2
    (early,) = hidden_units((own, own_l, own_r, below, above, far), weights)
    far_l, far_r = lax.optimization_barrier((shift(far, 1, 0), shift(far, -1, 0)))
    near_l, near_r, early = lax.optimization_barrier((near_l, near_r, early))
    two_up = shift(jnp.concatenate([near_l[:n], own_l[:, :h]], 1), 1, 0)
    two_down = shift(jnp.concatenate([near_r[n:], own_r[:, h:]], 1), -1, 0)
    far_2up, far_2down = shift(far_l[:, :h], 1, 0), shift(far_r[:, h:], -1, 0)
    late, down_v = hidden_units((near_l, near_r, far_l, far_r), weights, down_weight)
    two_up, two_down = two_hops(two_up, two_down, far_2up, far_2down, weights, down_v)
    return *other_terms(early, late, down_v), two_up, two_down


def returned(own_here, own_left, own_right, near_here, far_here, near_left, near_right, far_left, far_right, two_up, two_down):
    n, d = own_here.shape
    h = d // 2
    two_up, two_down = lax.optimization_barrier((shift(two_up, 1, 0), shift(two_down, -1, 0)))
    far_up, far_down = two_up[:, d + h :], two_down[:, d + h :]
    far_right = jnp.concatenate([b16(far_right[:, :h] + f32(far_up)), b16(far_right[:, h:])], 1)
    far_left = jnp.concatenate([b16(far_left[:, :h]), b16(far_left[:, h:] + f32(far_down))], 1)
    far_p, far_m = shift(far_right, 1, 0), shift(far_left, -1, 0)
    near_right = jnp.concatenate([b16(near_right[:n] + f32(two_up[:, :d])), b16(near_right[n:])], 0)
    near_left = jnp.concatenate([b16(near_left[:n]), b16(near_left[n:] + f32(two_down[:, :d]))], 0)
    near_p, near_m = shift(near_right, 1, 0), shift(near_left, -1, 0)
    own_right = jnp.concatenate([b16(own_right[:, :h] + f32(two_up[:, d : d + h])), b16(own_right[:, h:])], 1)
    own_left = jnp.concatenate([b16(own_left[:, :h]), b16(own_left[:, h:] + f32(two_down[:, d : d + h]))], 1)
    own_right, own_left, near_p, near_m = lax.optimization_barrier((own_right, own_left, near_p, near_m))
    far_sum = shift(b16(far_here + f32(far_p) + f32(far_m)), 0, 2)
    own_p, own_m = shift(own_right, 1, 0), shift(own_left, -1, 0)
    near_sum = b16(near_here + f32(near_p) + f32(near_m))
    from_below, from_above = shift(near_sum[n:], 0, 1), shift(near_sum[:n], 0, -1)
    return own_here + f32(own_p) + f32(own_m) + f32(far_sum) + f32(from_below) + f32(from_above)


def on_device(tokens, norm_gain, gate_weight, up_weight, down_weight):
    own = rms_normed(tokens, norm_gain)
    return b16(f32(tokens) + returned(*terms_of(own, gate_weight, up_weight, down_weight)))


def solution(mesh):
    return jax.shard_map(
        on_device,
        mesh=mesh,
        in_specs=(
            P(("dp", "tensor"), None),
            P(),
            P(None, "tensor"),
            P(None, "tensor"),
            P("tensor", None),
        ),
        out_specs=P(("dp", "tensor"), None),
        check_vma=False,
    )
```
